32 devices in a mesh: dp: 4 (over y, core), mp: 8 (over z, x).
Axes of the slice: x: 2, y: 2, z: 4, core: 2. Of those that a mesh axis runs over, the one named last changes fastest.
Arguments:
- tokens: bfloat16 [1024, 1024], P('dp'), may hold values from -6 to 6
- lengths: int32 [4], P('dp'), may hold values from 64 to 256
- cotangent: bfloat16 [1024, 1024], P('dp'), may hold values from -6 to 6
- triple_weight: bfloat16 [2, 1024, 3, 1024], P(None, None, None, 'mp'), may hold values from -0.1875 to 0.1875
- output_weight: bfloat16 [2, 1024, 1024], P(None, None, 'mp'), may hold values from -0.1875 to 0.1875
- upward_weight: bfloat16 [2, 1024, 4096], P(None, None, 'mp'), may hold values from -0.1875 to 0.1875
- downward_weight: bfloat16 [2, 1024, 4096], P(None, None, 'mp'), may hold values from -0.09375 to 0.09375
Outputs:
- final_stream: bfloat16 [1024, 1024], P('dp')
- triple_grad: float32 [2, 1024, 3, 1024], P(None, 'dp', None, 'mp')
- output_grad: float32 [2, 1024, 1024], P(None, 'dp', 'mp')
- upward_grad: float32 [2, 1024, 4096], P(None, 'dp', 'mp')
- downward_grad: float32 [2, 1024, 4096], P(None, 'dp', 'mp')
The draws below stay inside these ranges and needn't reach their ends.
Inputs may be any that keep to these rules, and one draw needn't show every extreme that they name: lengths[s] counts the live candidates of slate s; its other positions are padding.
All inputs are finite; a program needn't handle non-finite values.
Results may differ from the reference program's by a relative error of at most 0.04.
Values may be sent and summed in bfloat16 or wider, within the bound.
A program may use at most 64 MiB of HBM per device.

```python
import jax
import jax.numpy as jnp
from jax import lax

D = 1024
HEADS = 16
FF = 4096
HD = 64
SLATE = 256
LAYERS = 2
TOKENS = 1024
SLATES = 4
N_MP = 8


def place_ends(values, key, smallest, high):
    spot = [jax.random.randint(jax.random.fold_in(key, axis), (), 0, length) for axis, length in enumerate(values.shape)]
    widest = values.shape.index(max(values.shape))
    next_to = spot[:widest] + [(spot[widest] + 1) % values.shape[widest]] + spot[widest + 1:]
    return values.at[tuple(spot)].set(smallest).at[tuple(next_to)].set(high)


def levels(own_key, dims, shards, low, top_value):
    def one(dim, parts):
        draws = jax.random.uniform(jax.random.fold_in(jax.random.fold_in(own_key, 6), dim), (parts,), jnp.float32, low / len(shards), top_value / len(shards))
        return jnp.repeat(jnp.exp(draws), dims[dim] // parts).reshape((-1,) + (1,) * (len(dims) - dim - 1))

    gain = one(*shards[0])
    for cut in shards[1:]:
        gain = gain * one(*cut)
    return gain


def noise(key, shape, width, reach, pieces=(), held_as=jnp.bfloat16):
    drawn = jax.random.normal(key, shape, jnp.float32) * width
    if len(pieces) > 0:
        drawn = levels(key, shape, pieces, -0.22, 0.18) * drawn
    return jnp.clip(drawn, min=-reach, max=reach).astype(held_as)


def setup_inputs(seed: int = 0) -> dict:
    keys = jax.random.split(jax.random.key(seed), 8)
    tokens = noise(keys[0], (TOKENS, D), 1.0, 6.0, ((0, 4),))
    lengths = place_ends(jax.random.randint(keys[1], (SLATES,), SLATE // 4, SLATE + 1), jax.random.fold_in(keys[1], 1), SLATE // 4, SLATE).astype(jnp.int32)
    cotangent = noise(keys[2], (TOKENS, D), 1.0, 6.0, ((0, 4),))
    triple_weight = noise(keys[3], (LAYERS, D, 3, D), D ** -0.5, 0.1875, ((3, 8),))
    output_weight = noise(keys[4], (LAYERS, D, D), D ** -0.5, 0.1875, ((2, 8),))
    upward_weight = noise(keys[5], (LAYERS, D, FF), D ** -0.5, 0.1875, ((2, 8),))
    downward_weight = noise(keys[6], (LAYERS, D, FF), FF ** -0.5, 0.09375, ((2, 8),))
    return dict(tokens=tokens, lengths=lengths, cotangent=cotangent, triple_weight=triple_weight, output_weight=output_weight, upward_weight=upward_weight, downward_weight=downward_weight)


epsilon = 1e-06

def normalize(stream):
    widened = stream.astype(jnp.float32)
    rscale = lax.rsqrt(lax.optimization_barrier(jnp.mean(widened * widened, axis=-1, keepdims=True)) + epsilon)
    scaled = widened * rscale
    return (scaled.astype(jnp.bfloat16), scaled, rscale)

def norm_backward(scaled, rscale, upward):
    inner = lax.optimization_barrier(jnp.mean(upward * scaled, axis=-1, keepdims=True))
    return rscale * (upward - scaled * inner)

def smooth_gate(preact):
    return jax.nn.gelu(preact, approximate=True)

def attend(queries, key_rows, values, lengths):
    live_keys = (jnp.arange(SLATE)[None, :] < lengths[:, None]).astype(jnp.float32)
    scores = jnp.einsum('bqhe,bkhe->bhqk', queries.astype(jnp.float32), key_rows.astype(jnp.float32)) * HD ** (-0.5)
    weights = jnp.exp(scores) * live_keys[:, None, None, :]
    probs = weights / lax.optimization_barrier(jnp.sum(weights, axis=-1, keepdims=True))
    probs_low = probs.astype(jnp.bfloat16)
    context = jnp.einsum('bhqk,bkhe->bqhe', probs_low.astype(jnp.float32), values.astype(jnp.float32)).astype(jnp.bfloat16)
    return (probs, probs_low, context)

def attend_backward(probs, probs_low, queries, key_rows, values, grad_context):
    grad_prob = jnp.einsum('bqhe,bkhe->bhqk', grad_context.astype(jnp.float32), values.astype(jnp.float32))
    grad_value = jnp.einsum('bhqk,bqhe->bkhe', probs_low.astype(jnp.float32), grad_context.astype(jnp.float32)).astype(jnp.bfloat16)
    inner = lax.optimization_barrier(jnp.sum(grad_prob * probs, axis=-1, keepdims=True))
    grad_score = (probs * (grad_prob - inner) * HD ** (-0.5)).astype(jnp.bfloat16)
    grad_query = jnp.einsum('bhqk,bkhe->bqhe', grad_score.astype(jnp.float32), key_rows.astype(jnp.float32)).astype(jnp.bfloat16)
    grad_key = jnp.einsum('bhqk,bqhe->bkhe', grad_score.astype(jnp.float32), queries.astype(jnp.float32)).astype(jnp.bfloat16)
    return (grad_query, grad_key, grad_value)

def contract_rows(left, right):
    return lax.dot_general(left, right, (((0,), (0,)), ((), ())), preferred_element_type=jnp.float32)

def split_groups(matrix):
    return jnp.moveaxis(matrix.reshape(matrix.shape[0], N_MP, -1), 1, 0)

def split_triples(matrix):
    leading = matrix.shape[0]
    return matrix.reshape(leading, 3, N_MP, -1).transpose(2, 0, 1, 3).reshape(N_MP, leading, -1)

def group_total(left_parts, right_parts):

    def add_group(running, operands):
        addend = lax.dot_general(operands[0], operands[1], (((1,), (1,)), ((), ())), preferred_element_type=jnp.float32)
        return (running + lax.optimization_barrier(addend.astype(jnp.bfloat16)).astype(jnp.float32), None)
    start_value = jnp.zeros((left_parts.shape[1], right_parts.shape[1]), jnp.float32)
    running, _ = lax.scan(add_group, start_value, (left_parts, right_parts))
    return running

def reference(tokens, lengths, cotangent, triple_weight, output_weight, upward_weight, downward_weight):
    row_count = tokens.shape[0]
    slates = row_count // SLATE
    model_width = tokens.shape[1]
    stream = tokens
    saved = []
    for layer_index in range(LAYERS):
        normed, scaled, rscale = normalize(stream)
        flat_triple = triple_weight[layer_index].reshape(model_width, -1)
        qkv = jnp.dot(normed, flat_triple, preferred_element_type=jnp.float32).astype(jnp.bfloat16)
        shaped = qkv.reshape(slates, SLATE, 3, HEADS, HD)
        queries = shaped[:, :, 0]
        key_rows = shaped[:, :, 1]
        values = shaped[:, :, 2]
        probs, probs_low, context = attend(queries, key_rows, values, lengths)
        context_flat = context.reshape(row_count, -1)
        attn_sum = group_total(split_groups(context_flat), split_groups(output_weight[layer_index]))
        mid_stream = (stream.astype(jnp.float32) + attn_sum).astype(jnp.bfloat16)
        normed_mid, scaled_mid, rscale_mid = normalize(mid_stream)
        preact = jnp.dot(normed_mid, upward_weight[layer_index], preferred_element_type=jnp.float32)
        activated = smooth_gate(preact).astype(jnp.bfloat16)
        ffn_sum = group_total(split_groups(activated), split_groups(downward_weight[layer_index]))
        stream = (mid_stream.astype(jnp.float32) + ffn_sum).astype(jnp.bfloat16)
        saved.append((normed, scaled, rscale, queries, key_rows, values, probs, probs_low, context_flat, scaled_mid, rscale_mid, normed_mid, preact, activated))
    final_stream = stream
    gradients = []
    upstream = cotangent
    for layer_index in reversed(range(LAYERS)):
        normed, scaled, rscale, queries, key_rows, values, probs, probs_low, context_flat, scaled_mid, rscale_mid, normed_mid, preact, activated = saved[layer_index]
        downward_grad = contract_rows(upstream, activated)
        grad_act = jnp.dot(upstream, downward_weight[layer_index], preferred_element_type=jnp.float32).astype(jnp.bfloat16)
        _, gate_back = jax.vjp(smooth_gate, preact)
        grad_preact = gate_back(grad_act.astype(jnp.float32))[0].astype(jnp.bfloat16)
        upward_grad = contract_rows(normed_mid, grad_preact)
        grad_normed = group_total(split_groups(grad_preact), split_groups(upward_weight[layer_index]))
        grad_mid = (upstream.astype(jnp.float32) + norm_backward(scaled_mid, rscale_mid, grad_normed)).astype(jnp.bfloat16)
        output_grad = contract_rows(grad_mid, context_flat)
        grad_context = jnp.dot(grad_mid, output_weight[layer_index], preferred_element_type=jnp.float32).astype(jnp.bfloat16)
        grad_query, grad_key, grad_value = attend_backward(probs, probs_low, queries, key_rows, values, grad_context.reshape(slates, SLATE, HEADS, HD))
        grad_qkv = jnp.stack([grad_query, grad_key, grad_value], axis=2).reshape(row_count, -1)
        triple_grad = contract_rows(normed, grad_qkv).reshape(model_width, 3, -1)
        gradients.insert(0, (triple_grad, output_grad, upward_grad, downward_grad))
        if layer_index > 0:
            grad_input = group_total(split_triples(grad_qkv), split_triples(triple_weight[layer_index]))
            upstream = (grad_mid.astype(jnp.float32) + norm_backward(scaled, rscale, grad_input)).astype(jnp.bfloat16)
    merged = [jnp.stack([gradients[layer_pos][slot_index] for layer_pos in range(LAYERS)]) for slot_index in range(4)]
    return (final_stream, merged[0], merged[1], merged[2], merged[3])
```

```python
import functools

import jax
import jax.numpy as jnp
from jax import lax
from jax.experimental import pallas as pl
from jax.experimental.pallas import tpu as pltpu
from jax.sharding import PartitionSpec as P

HD = 64
SLATE = 256
LAYERS = 2
MESH = pl.DeviceIdType.MESH


epsilon = 1e-06


def normalize(stream):
    widened = stream.astype(jnp.float32)
    rscale = lax.rsqrt(jnp.mean(widened * widened, axis=-1, keepdims=True) + epsilon)
    scaled = widened * rscale
    return (scaled.astype(jnp.bfloat16), scaled, rscale)


def norm_backward(scaled, rscale, upward):
    inner = jnp.mean(upward * scaled, axis=-1, keepdims=True)
    return rscale * (upward - scaled * inner)


def smooth_gate(preact):
    return jax.nn.gelu(preact, approximate=True)


def attend(queries, key_rows, values, lengths):
    live_keys = (jnp.arange(SLATE)[None, :] < lengths[:, None]).astype(jnp.float32)
    scores = jnp.einsum(
        "bqhe,bkhe->bhqk", queries, key_rows, preferred_element_type=jnp.float32
    ) * HD ** (-0.5)
    weights = jnp.exp(scores) * live_keys[:, None, None, :]
    probs = weights / jnp.sum(weights, axis=-1, keepdims=True)
    probs_low = probs.astype(jnp.bfloat16)
    context = jnp.einsum(
        "bhqk,bkhe->bqhe", probs_low, values, preferred_element_type=jnp.float32
    ).astype(jnp.bfloat16)
    return (probs, probs_low, context)


def attend_backward(probs, probs_low, queries, key_rows, values, grad_context):
    grad_prob = jnp.einsum(
        "bqhe,bkhe->bhqk", grad_context, values, preferred_element_type=jnp.float32
    )
    grad_value = jnp.einsum(
        "bhqk,bqhe->bkhe", probs_low, grad_context, preferred_element_type=jnp.float32
    ).astype(jnp.bfloat16)
    inner = jnp.sum(grad_prob * probs, axis=-1, keepdims=True)
    grad_score = (probs * (grad_prob - inner) * HD ** (-0.5)).astype(jnp.bfloat16)
    grad_query = jnp.einsum(
        "bhqk,bkhe->bqhe", grad_score, key_rows, preferred_element_type=jnp.float32
    ).astype(jnp.bfloat16)
    grad_key = jnp.einsum(
        "bhqk,bqhe->bkhe", grad_score, queries, preferred_element_type=jnp.float32
    ).astype(jnp.bfloat16)
    return (grad_query, grad_key, grad_value)


def contract_rows(left, right):
    return lax.dot_general(
        left, right, (((0,), (0,)), ((), ())), preferred_element_type=jnp.float32
    )


def contract_cols(left, right):
    return lax.dot_general(
        left, right, (((1,), (1,)), ((), ())), preferred_element_type=jnp.float32
    )


def remote(src, dst, send_sem, recv_sem, axis, device):
    return pltpu.make_async_remote_copy(
        src_ref=src,
        dst_ref=dst,
        send_sem=send_sem,
        recv_sem=recv_sem,
        device_id={axis: device},
        device_id_type=MESH,
    )


def place(axis, n):
    me = lax.axis_index(axis)
    parity = lax.rem(me, 2)
    group = lax.div(me, 2)
    partner = me + 1 - 2 * parity
    groups = n // 2
    return me, parity, group, partner, groups


def greet(axis, n):
    me, parity, group, partner, groups = place(axis, n)
    barrier = pltpu.get_barrier_semaphore()
    pl.semaphore_signal(barrier, inc=1, device_id={axis: partner}, device_id_type=MESH)
    for j in range(1, groups):
        peer = lax.rem(group + j, groups) * 2 + parity
        pl.semaphore_signal(barrier, inc=1, device_id={axis: peer}, device_id_type=MESH)
    return groups


def sum_scatter(axis, n, part, first, held, second, sems):
    me, parity, group, partner, groups = place(axis, n)
    to_pair, to_peer = [None] * groups, [None] * groups
    order = list(range(1, groups)) + [0]
    for j in order:
        there = lax.rem(group + j, groups) * 2
        to_pair[j] = remote(
            part.at[there + 1 - parity], first.at[j], sems.at[0, j], sems.at[1, j], axis, partner
        )
        to_pair[j].start()
    for j in order[:-1]:
        peer = lax.rem(group + j, groups) * 2 + parity
        to_pair[j].wait_recv()
        held[j] = (part[peer].astype(jnp.float32) + first[j].astype(jnp.float32)).astype(held.dtype)
        to_peer[j] = remote(held.at[j], second.at[j], sems.at[2, j], sems.at[3, j], axis, peer)
        to_peer[j].start()
    to_pair[0].wait_recv()
    total = part[me].astype(jnp.float32) + first[0].astype(jnp.float32)
    for j in order[:-1]:
        to_peer[j].wait_recv()
        total = total + second[j].astype(jnp.float32)
    return total, to_pair + to_peer[1:]


def spread(axis, n, whole, sems):
    me, parity, group, partner, groups = place(axis, n)
    sent = []
    for j in range(1, groups):
        peer = lax.rem(group + j, groups) * 2 + parity
        copy = remote(whole.at[me], whole.at[me], sems.at[4, j], sems.at[5, j], axis, peer)
        copy.start()
        sent.append(copy)
    across = [remote(whole.at[me], whole.at[me], sems.at[6, 0], sems.at[7, 0], axis, partner)]
    across[0].start()
    for j in range(1, groups):
        sent[j - 1].wait_recv()
        owner = lax.rem(group + groups - j, groups) * 2 + parity
        copy = remote(whole.at[owner], whole.at[owner], sems.at[6, j], sems.at[7, j], axis, partner)
        copy.start()
        across.append(copy)
    for copy in across:
        copy.wait_recv()
    return sent + across


def forward_sum(n, part, stream, out, first, held, second, whole, sems):
    me = lax.axis_index("mp")
    pl.semaphore_wait(pltpu.get_barrier_semaphore(), greet("mp", n))
    total, copies = sum_scatter("mp", n, part, first, held, second, sems)
    whole[me] = (stream[me].astype(jnp.float32) + total).astype(whole.dtype)
    copies = copies + spread("mp", n, whole, sems)
    for copy in copies:
        copy.wait_send()
    out[...] = whole[...]


def backward_sum(n, part, stream, upstream, out, first, held, second, whole, sems):
    me = lax.axis_index("mp")
    pl.semaphore_wait(pltpu.get_barrier_semaphore(), greet("mp", n))
    total, copies = sum_scatter("mp", n, part, first, held, second, sems)
    _, scaled, rscale = normalize(stream[me])
    whole[me] = (
        upstream[me].astype(jnp.float32) + norm_backward(scaled, rscale, total)
    ).astype(whole.dtype)
    copies = copies + spread("mp", n, whole, sems)
    for copy in copies:
        copy.wait_send()
    out[...] = whole[...]


def summed(kernel, collective_id, n, part, *rest):
    rows, columns = part.shape
    chunk = rows // n
    cut = (n, chunk, columns)
    half = (n // 2, chunk, columns)
    vmem = pl.BlockSpec(memory_space=pltpu.VMEM)
    operands = [array.reshape(cut) for array in (part,) + rest]
    out = pl.pallas_call(
        functools.partial(kernel, n),
        out_shape=jax.ShapeDtypeStruct(cut, part.dtype),
        in_specs=[vmem] * len(operands),
        out_specs=vmem,
        scratch_shapes=[
            pltpu.VMEM(half, part.dtype),
            pltpu.VMEM(half, part.dtype),
            pltpu.VMEM(half, part.dtype),
            pltpu.VMEM(cut, part.dtype),
            pltpu.SemaphoreType.DMA((8, n // 2)),
        ],
        compiler_params=pltpu.CompilerParams(
            collective_id=collective_id, has_side_effects=True, vmem_limit_bytes=16 << 20
        ),
    )(*operands)
    return out.reshape(rows, columns)


def body(n, tokens, lengths, cotangent, triple_weight, output_weight, upward_weight, downward_weight):
    row_count = tokens.shape[0]
    slates = row_count // SLATE
    model_width = tokens.shape[1]
    heads_here = triple_weight.shape[-1] // HD
    stream = tokens
    saved = []
    for layer_index in range(LAYERS):
        normed, _, _ = normalize(stream)
        flat_triple = triple_weight[layer_index].reshape(model_width, -1)
        qkv = jnp.dot(normed, flat_triple, preferred_element_type=jnp.float32).astype(jnp.bfloat16)
        shaped = qkv.reshape(slates, SLATE, 3, heads_here, HD)
        queries = shaped[:, :, 0]
        key_rows = shaped[:, :, 1]
        values = shaped[:, :, 2]
        probs, probs_low, context = attend(queries, key_rows, values, lengths)
        context_flat = context.reshape(row_count, -1)
        partial_att = contract_cols(context_flat, output_weight[layer_index])
        mid_stream = summed(forward_sum, 0, n, partial_att.astype(jnp.bfloat16), stream)
        normed_mid, _, _ = normalize(mid_stream)
        preact = jnp.dot(normed_mid, upward_weight[layer_index], preferred_element_type=jnp.float32)
        activated = smooth_gate(preact).astype(jnp.bfloat16)
        partial_ffn = contract_cols(activated, downward_weight[layer_index])
        saved.append(
            (
                stream,
                normed,
                queries,
                key_rows,
                values,
                probs,
                probs_low,
                context_flat,
                mid_stream,
                normed_mid,
                preact,
                activated,
            )
        )
        stream = summed(forward_sum, 0, n, partial_ffn.astype(jnp.bfloat16), mid_stream)
    final_stream = stream
    gradients = []
    upstream = cotangent
    for layer_index in reversed(range(LAYERS)):
        (
            stream,
            normed,
            queries,
            key_rows,
            values,
            probs,
            probs_low,
            context_flat,
            mid_stream,
            normed_mid,
            preact,
            activated,
        ) = saved[layer_index]
        downward_grad = contract_rows(upstream, activated)
        grad_act = jnp.dot(
            upstream, downward_weight[layer_index], preferred_element_type=jnp.float32
        ).astype(jnp.bfloat16)
        _, gate_back = jax.vjp(smooth_gate, preact)
        grad_preact = gate_back(grad_act.astype(jnp.float32))[0].astype(jnp.bfloat16)
        upward_grad = contract_rows(normed_mid, grad_preact)
        grad_mid = summed(
            backward_sum,
            1,
            n,
            contract_cols(grad_preact, upward_weight[layer_index]).astype(jnp.bfloat16),
            mid_stream,
            upstream,
        )
        output_grad = contract_rows(grad_mid, context_flat)
        grad_context = jnp.dot(
            grad_mid, output_weight[layer_index], preferred_element_type=jnp.float32
        ).astype(jnp.bfloat16)
        grad_query, grad_key, grad_value = attend_backward(
            probs,
            probs_low,
            queries,
            key_rows,
            values,
            grad_context.reshape(slates, SLATE, heads_here, HD),
        )
        grad_qkv = jnp.stack([grad_query, grad_key, grad_value], axis=2).reshape(row_count, -1)
        triple_grad = contract_rows(normed, grad_qkv)
        pieces = (triple_grad, output_grad, upward_grad, downward_grad)
        joined = jnp.concatenate([piece.astype(jnp.bfloat16) for piece in pieces], axis=1)
        shares = lax.psum_scatter(joined, "dp", scatter_dimension=0, tiled=True)
        cuts = [sum(piece.shape[1] for piece in pieces[:count]) for count in (1, 2, 3)]
        gradients.insert(0, jnp.split(shares, cuts, axis=1))
        if layer_index > 0:
            flat_triple = triple_weight[layer_index].reshape(model_width, -1)
            upstream = summed(
                backward_sum,
                1,
                n,
                contract_cols(grad_qkv, flat_triple).astype(jnp.bfloat16),
                stream,
                grad_mid,
            )
    merged = [
        jnp.stack([gradients[layer_pos][slot_index] for layer_pos in range(LAYERS)]).astype(jnp.float32)
        for slot_index in range(4)
    ]
    triple = merged[0].reshape(LAYERS, merged[0].shape[1], 3, -1)
    return (final_stream, triple, merged[1], merged[2], merged[3])


def solution(mesh):
    placed = (
        P("dp", None),
        P("dp"),
        P("dp", None),
        P(None, None, None, "mp"),
        P(None, None, "mp"),
        P(None, None, "mp"),
        P(None, None, "mp"),
    )
    return jax.shard_map(
        functools.partial(body, mesh.shape["mp"]),
        mesh=mesh,
        in_specs=placed,
        out_specs=(
            P("dp", None),
            P(None, "dp", None, "mp"),
            P(None, "dp", "mp"),
            P(None, "dp", "mp"),
            P(None, "dp", "mp"),
        ),
        check_vma=False,
    )
```

```python
import functools

import jax
import jax.numpy as jnp
from jax import lax
from jax.experimental import pallas as pl
from jax.experimental.pallas import tpu as pltpu
from jax.sharding import PartitionSpec as P

HD = 64
SLATE = 256
LAYERS = 2
MESH = pl.DeviceIdType.MESH


epsilon = 1e-06


def normalize(stream):
    widened = stream.astype(jnp.float32)
    rscale = lax.rsqrt(jnp.mean(widened * widened, axis=-1, keepdims=True) + epsilon)
    scaled = widened * rscale
    return (scaled.astype(jnp.bfloat16), scaled, rscale)


def norm_backward(scaled, rscale, upward):
    inner = jnp.mean(upward * scaled, axis=-1, keepdims=True)
    return rscale * (upward - scaled * inner)


def contract_rows(left, right):
    return lax.dot_general(
        left, right, (((0,), (0,)), ((), ())), preferred_element_type=jnp.float32
    )


def contract_cols(left, right):
    return lax.dot_general(
        left, right, (((1,), (1,)), ((), ())), preferred_element_type=jnp.float32
    )


def remote(src, dst, send_sem, recv_sem, axis, device):
    return pltpu.make_async_remote_copy(
        src_ref=src,
        dst_ref=dst,
        send_sem=send_sem,
        recv_sem=recv_sem,
        device_id={axis: device},
        device_id_type=MESH,
    )


def place(axis, n):
    me = lax.axis_index(axis)
    parity = lax.rem(me, 2)
    group = lax.div(me, 2)
    partner = me + 1 - 2 * parity
    groups = n // 2
    return me, parity, group, partner, groups


ROOT = (2.0 / 3.141592653589793) ** 0.5
CUBIC = 0.044715


def gate(preact):
    bent = jnp.tanh(ROOT * (preact + CUBIC * (preact * preact * preact)))
    return 0.5 * preact * (1.0 + bent)


def gate_slope(preact):
    square = preact * preact
    bent = jnp.tanh(ROOT * (preact + CUBIC * (square * preact)))
    inner = ROOT * (1.0 + 3.0 * CUBIC * square)
    return 0.5 * (1.0 + bent) + 0.5 * preact * (1.0 - bent * bent) * inner


def dot(left, right):
    return jnp.dot(left, right, preferred_element_type=jnp.float32)


def low(value):
    return value.astype(jnp.bfloat16)


def wide(value):
    return value.astype(jnp.float32)


class Scatter:
    def __init__(self, axis, n, part, first, held, second, sems):
        self.axis, self.n = axis, n
        self.part, self.first, self.held, self.second, self.sems = part, first, held, second, sems
        self.me, self.parity, self.group, self.partner, self.groups = place(axis, n)
        self.order = list(range(1, self.groups)) + [0]
        self.copies = []

    def peer(self, j):
        return lax.rem(self.group + j, self.groups) * 2 + self.parity

    def start(self):
        self.to_pair = [None] * self.groups
        for j in self.order:
            theirs = lax.rem(self.group + j, self.groups) * 2 + 1 - self.parity
            self.to_pair[j] = remote(
                self.part.at[theirs],
                self.first.at[j],
                self.sems.at[0, j],
                self.sems.at[1, j],
                self.axis,
                self.partner,
            )
            self.to_pair[j].start()
        self.copies += self.to_pair

    def pass_on(self):
        self.to_peer = []
        for j in self.order[:-1]:
            peer = self.peer(j)
            self.to_pair[j].wait_recv()
            self.held[j] = low(wide(self.part[peer]) + wide(self.first[j]))
            copy = remote(
                self.held.at[j],
                self.second.at[j],
                self.sems.at[2, j],
                self.sems.at[3, j],
                self.axis,
                peer,
            )
            copy.start()
            self.to_peer.append(copy)
        self.copies += self.to_peer

    def total(self):
        self.to_pair[0].wait_recv()
        total = wide(self.part[self.me]) + wide(self.first[0])
        for j in self.order[:-1]:
            self.to_peer[j - 1].wait_recv()
            total = total + wide(self.second[j])
        return total

    def drain(self):
        for copy in self.copies:
            copy.wait_send()


class Reduce(Scatter):
    def __init__(self, axis, n, part, first, held, second, whole, sems):
        super().__init__(axis, n, part, first, held, second, sems)
        self.whole = whole

    def gather(self):
        mine = self.whole.at[self.me]
        self.around = []
        for j in range(1, self.groups):
            self.around.append(
                remote(mine, mine, self.sems.at[4, j], self.sems.at[5, j], self.axis, self.peer(j))
            )
            self.around[-1].start()
        across = remote(mine, mine, self.sems.at[6, 0], self.sems.at[7, 0], self.axis, self.partner)
        across.start()
        self.across = [across]

    def forward(self):
        for j in range(1, self.groups):
            self.around[j - 1].wait_recv()
            owner = lax.rem(self.group + self.groups - j, self.groups) * 2 + self.parity
            block = self.whole.at[owner]
            copy = remote(
                block, block, self.sems.at[6, j], self.sems.at[7, j], self.axis, self.partner
            )
            copy.start()
            self.across.append(copy)

    def finish(self):
        for copy in self.across:
            copy.wait_recv()
        self.copies += self.around + self.across


def greet(axes):
    barrier = pltpu.get_barrier_semaphore()
    count = 0
    for axis, n in axes:
        _, parity, group, partner, groups = place(axis, n)
        others = [partner]
        for j in range(1, groups):
            others.append(lax.rem(group + j, groups) * 2 + parity)
        for other in others:
            pl.semaphore_signal(barrier, inc=1, device_id={axis: other}, device_id_type=MESH)
        count += len(others)
    pl.semaphore_wait(barrier, count)


def kernel(
    n,
    m,
    lengths,
    tokens,
    cotangent,
    triple_weight,
    output_weight,
    upward_weight,
    downward_weight,
    final_out,
    triple_out,
    output_out,
    upward_out,
    downward_out,
    part,
    first,
    held,
    second,
    whole,
    sems,
    ffn_part,
    ffn_first,
    ffn_held,
    ffn_second,
    ffn_sems,
    out_part,
    out_first,
    out_held,
    out_second,
    out_sems,
    qkv_part,
    qkv_first,
    qkv_held,
    qkv_second,
    qkv_sems,
    normed,
    qkv,
    probs,
    context,
    normed_mid,
    slope,
    activated,
    grad_act,
    grad_qkv,
):
    greet((("mp", n), ("dp", m)))
    _, chunk, width = tokens.shape
    row_count = n * chunk
    slates = row_count // SLATE
    held_cols = output_weight.shape[-1]
    heads = held_cols // HD
    hidden = upward_weight.shape[-1]
    me = lax.axis_index("mp")
    position = lax.broadcasted_iota(jnp.int32, (1, SLATE), 1)

    def rows(ref):
        return ref[...].reshape(row_count, width)

    def reducer(k):
        return Reduce(
            "mp", n, part.at[k], first.at[k], held.at[k], second.at[k], whole.at[k], sems.at[k]
        )

    def put(k, value):
        part[k] = low(value).reshape(n, chunk, width)

    def scatterer(refs, l):
        return Scatter("dp", m, *[ref.at[l] for ref in refs])

    def put_grad(ref, l, start, value):
        columns = value.shape[1]
        ref[l, :, :, start : start + columns] = low(value).reshape(m, -1, columns)

    def slices(s, h):
        block = slice(s * SLATE, (s + 1) * SLATE)
        return block, [slice(i * held_cols + h * HD, i * held_cols + (h + 1) * HD) for i in range(3)]

    drained = []
    stream = tokens
    streams, mids = [], []
    for l in range(LAYERS):
        last = l == LAYERS - 1
        streams.append(stream)
        normed[l] = normalize(rows(stream))[0]
        qkv[l] = low(dot(normed[l], triple_weight[l]))
        for s in range(slates):
            live = wide(position < lengths[s])
            for h in range(heads):
                block, (q, k, v) = slices(s, h)
                scores = contract_cols(qkv[l, block, q], qkv[l, block, k]) * HD ** (-0.5)
                weights = jnp.exp(scores) * live
                share = weights / jnp.sum(weights, axis=-1, keepdims=True)
                probs[l, s * heads + h] = share
                context[l, block, h * HD : (h + 1) * HD] = low(dot(low(share), qkv[l, block, v]))
        step = reducer(2 * l)
        put(2 * l, contract_cols(context[l], output_weight[l]))
        step.start()
        if l == 0:
            grad_act[...] = low(dot(rows(cotangent), downward_weight[LAYERS - 1]))
        step.pass_on()
        whole[2 * l, me] = low(wide(stream[me]) + step.total())
        step.gather()
        step.forward()
        step.finish()
        drained.append(step)
        mid = whole.at[2 * l]
        mids.append(mid)
        normed_mid[l] = normalize(rows(mid))[0]
        preact = dot(normed_mid[l], upward_weight[l])
        activated[l] = low(gate(preact))
        if not last:
            put(2 * l + 1, contract_cols(activated[l], downward_weight[l]))
            step = reducer(2 * l + 1)
            step.start()
            slope[l] = gate_slope(preact)
            step.pass_on()
            whole[2 * l + 1, me] = low(wide(mid[me]) + step.total())
            step.gather()
            step.forward()
            step.finish()
            drained.append(step)
            stream = whole.at[2 * l + 1]
        else:
            slope[l] = gate_slope(preact)

    final_k = 2 * LAYERS - 1
    final = reducer(final_k)

    def final_gather():
        whole[final_k, me] = low(wide(mids[-1][me]) + final.total())
        final.gather()

    def final_finish():
        final.finish()
        final_out[...] = whole[final_k]

    later = [final.start, final.pass_on, final_gather, final.forward, final_finish]

    def advance():
        if later:
            later.pop(0)()

    pending = []

    def flush():
        while pending:
            pending.pop(0)()

    def ffn_done(scatter, l):
        total = scatter.total()
        downward_out[l] = total[:, :hidden]
        upward_out[l] = total[:, hidden:]

    def out_done(scatter, l):
        output_out[l] = scatter.total()

    def qkv_done(scatter, l):
        triple_out[l] = scatter.total()

    upstream = cotangent
    k_next = 2 * LAYERS
    for l in reversed(range(LAYERS)):
        if l == LAYERS - 1:
            act_back = grad_act[...]
        else:
            act_back = low(dot(rows(upstream), downward_weight[l]))
        grad_preact = low(wide(act_back) * slope[l])
        step = reducer(k_next)
        put(k_next, contract_cols(grad_preact, upward_weight[l]))
        step.start()
        ffn = scatterer((ffn_part, ffn_first, ffn_held, ffn_second, ffn_sems), l)
        put_grad(ffn_part, l, 0, contract_rows(rows(upstream), activated[l]))
        step.pass_on()
        put_grad(ffn_part, l, hidden, contract_rows(normed_mid[l], grad_preact))
        ffn.start()
        if l == LAYERS - 1:
            put(final_k, contract_cols(activated[l], downward_weight[l]))
        _, scaled, rscale = normalize(mids[l][me])
        whole[k_next, me] = low(wide(upstream[me]) + norm_backward(scaled, rscale, step.total()))
        step.gather()
        flush()
        ffn.pass_on()
        step.forward()
        step.finish()
        advance()
        drained += [step, ffn]
        grad_mid = whole.at[k_next]
        k_next += 1
        put_grad(out_part, l, 0, contract_rows(rows(grad_mid), context[l]))
        out = scatterer((out_part, out_first, out_held, out_second, out_sems), l)
        out.start()
        grad_context = low(dot(rows(grad_mid), output_weight[l]))
        for s in range(slates):
            for h in range(heads):
                block, (q, k, v) = slices(s, h)
                share = probs[l, s * heads + h]
                back = grad_context[block, h * HD : (h + 1) * HD]
                grad_prob = contract_cols(back, qkv[l, block, v])
                grad_qkv[l, block, v] = low(contract_rows(low(share), back))
                inner = jnp.sum(grad_prob * share, axis=-1, keepdims=True)
                grad_score = low(share * (grad_prob - inner) * HD ** (-0.5))
                grad_qkv[l, block, q] = low(dot(grad_score, qkv[l, block, k]))
                grad_qkv[l, block, k] = low(contract_rows(grad_score, qkv[l, block, q]))
        triple = scatterer((qkv_part, qkv_first, qkv_held, qkv_second, qkv_sems), l)
        drained += [out, triple]
        if l > 0:
            step = reducer(k_next)
            put(k_next, contract_cols(grad_qkv[l], triple_weight[l]))
            step.start()
            out.pass_on()
            put_grad(qkv_part, l, 0, contract_rows(normed[l], grad_qkv[l]))
            step.pass_on()
            triple.start()
            _, scaled, rscale = normalize(streams[l][me])
            whole[k_next, me] = low(
                wide(grad_mid[me]) + norm_backward(scaled, rscale, step.total())
            )
            step.gather()
            ffn_done(ffn, l)
            triple.pass_on()
            step.forward()
            step.finish()
            advance()
            drained.append(step)
            upstream = whole.at[k_next]
            k_next += 1
            pending.append(functools.partial(out_done, out, l))
            pending.append(functools.partial(qkv_done, triple, l))
        else:
            put_grad(qkv_part, l, 0, contract_rows(normed[l], grad_qkv[l]))
            triple.start()
            out.pass_on()
            advance()
            triple.pass_on()
            advance()
            ffn_done(ffn, l)
            out_done(out, l)
            while later:
                advance()
            qkv_done(triple, l)
    drained.append(final)
    for item in drained:
        item.drain()


def body(
    n, m, tokens, lengths, cotangent, triple_weight, output_weight, upward_weight, downward_weight
):
    row_count, width = tokens.shape
    chunk = row_count // n
    share = width // m
    held_cols = output_weight.shape[-1]
    hidden = upward_weight.shape[-1]
    triple_cols = 3 * held_cols
    heads_all = (row_count // SLATE) * (held_cols // HD)
    sums = 2 * LAYERS + 2 * LAYERS - 1
    vmem = pl.BlockSpec(memory_space=pltpu.VMEM)
    smem = pl.BlockSpec(memory_space=pltpu.SMEM)
    bf16, f32 = jnp.bfloat16, jnp.float32

    def scratch(count, parts, rows, columns):
        half = pltpu.VMEM((count, parts // 2, rows, columns), bf16)
        return [pltpu.VMEM((count, parts, rows, columns), bf16), half, half, half]

    def sems(count, kinds, parts):
        return pltpu.SemaphoreType.DMA((count, kinds, parts // 2))

    outs = pl.pallas_call(
        functools.partial(kernel, n, m),
        out_shape=[
            jax.ShapeDtypeStruct((n, chunk, width), bf16),
            jax.ShapeDtypeStruct((LAYERS, share, triple_cols), f32),
            jax.ShapeDtypeStruct((LAYERS, share, held_cols), f32),
            jax.ShapeDtypeStruct((LAYERS, share, hidden), f32),
            jax.ShapeDtypeStruct((LAYERS, share, hidden), f32),
        ],
        in_specs=[smem] + [vmem] * 6,
        out_specs=[vmem] * 5,
        scratch_shapes=scratch(sums, n, chunk, width)
        + [pltpu.VMEM((sums, n, chunk, width), bf16), sems(sums, 8, n)]
        + scratch(LAYERS, m, share, 2 * hidden)
        + [sems(LAYERS, 4, m)]
        + scratch(LAYERS, m, share, held_cols)
        + [sems(LAYERS, 4, m)]
        + scratch(LAYERS, m, share, triple_cols)
        + [sems(LAYERS, 4, m)]
        + [
            pltpu.VMEM((LAYERS, row_count, width), bf16),
            pltpu.VMEM((LAYERS, row_count, triple_cols), bf16),
            pltpu.VMEM((LAYERS, heads_all, SLATE, SLATE), f32),
            pltpu.VMEM((LAYERS, row_count, held_cols), bf16),
            pltpu.VMEM((LAYERS, row_count, width), bf16),
            pltpu.VMEM((LAYERS, row_count, hidden), f32),
            pltpu.VMEM((LAYERS, row_count, hidden), bf16),
            pltpu.VMEM((row_count, hidden), bf16),
            pltpu.VMEM((LAYERS, row_count, triple_cols), bf16),
        ],
        compiler_params=pltpu.CompilerParams(
            collective_id=0, has_side_effects=True, vmem_limit_bytes=58 << 20
        ),
    )(
        lengths,
        tokens.reshape(n, chunk, width),
        cotangent.reshape(n, chunk, width),
        triple_weight.reshape(LAYERS, width, triple_cols),
        output_weight,
        upward_weight,
        downward_weight,
    )
    final, triple, output, upward, downward = outs
    return (
        final.reshape(row_count, width),
        triple.reshape(LAYERS, share, 3, held_cols),
        output,
        upward,
        downward,
    )


def solution(mesh):
    placed = (
        P("dp", None),
        P("dp"),
        P("dp", None),
        P(None, None, None, "mp"),
        P(None, None, "mp"),
        P(None, None, "mp"),
        P(None, None, "mp"),
    )
    return jax.shard_map(
        functools.partial(body, mesh.shape["mp"], mesh.shape["dp"]),
        mesh=mesh,
        in_specs=placed,
        out_specs=(
            P("dp", None),
            P(None, "dp", None, "mp"),
            P(None, "dp", "mp"),
            P(None, "dp", "mp"),
            P(None, "dp", "mp"),
        ),
        check_vma=False,
    )
```

```python
import functools

import jax
import jax.numpy as jnp
from jax import lax
from jax.experimental import pallas as pl
from jax.experimental.pallas import tpu as pltpu
from jax.sharding import PartitionSpec as P

HD = 64
SLATE = 256
LAYERS = 2
MESH = pl.DeviceIdType.MESH


epsilon = 1e-06


def normalize(stream):
    widened = stream.astype(jnp.float32)
    rscale = lax.rsqrt(jnp.mean(widened * widened, axis=-1, keepdims=True) + epsilon)
    scaled = widened * rscale
    return (scaled.astype(jnp.bfloat16), scaled, rscale)


def norm_backward(scaled, rscale, upward):
    inner = jnp.mean(upward * scaled, axis=-1, keepdims=True)
    return rscale * (upward - scaled * inner)


def contract_rows(left, right):
    return lax.dot_general(
        left, right, (((0,), (0,)), ((), ())), preferred_element_type=jnp.float32
    )


def contract_cols(left, right):
    return lax.dot_general(
        left, right, (((1,), (1,)), ((), ())), preferred_element_type=jnp.float32
    )


def remote(src, dst, send_sem, recv_sem, axis, device):
    return pltpu.make_async_remote_copy(
        src_ref=src,
        dst_ref=dst,
        send_sem=send_sem,
        recv_sem=recv_sem,
        device_id={axis: device},
        device_id_type=MESH,
    )


def place(axis, n):
    me = lax.axis_index(axis)
    parity = lax.rem(me, 2)
    group = lax.div(me, 2)
    partner = me + 1 - 2 * parity
    groups = n // 2
    return me, parity, group, partner, groups


ROOT = (2.0 / 3.141592653589793) ** 0.5
CUBIC = 0.044715


def gate(preact):
    bent = jnp.tanh(ROOT * (preact + CUBIC * (preact * preact * preact)))
    return 0.5 * preact * (1.0 + bent)


def gate_slope(preact):
    square = preact * preact
    bent = jnp.tanh(ROOT * (preact + CUBIC * (square * preact)))
    inner = ROOT * (1.0 + 3.0 * CUBIC * square)
    return 0.5 * (1.0 + bent) + 0.5 * preact * (1.0 - bent * bent) * inner


def dot(left, right):
    return jnp.dot(left, right, preferred_element_type=jnp.float32)


def low(value):
    return value.astype(jnp.bfloat16)


def wide(value):
    return value.astype(jnp.float32)


class Scatter:
    def __init__(self, axis, n, part, first, held, second, sems):
        self.axis, self.n = axis, n
        self.part, self.first, self.held, self.second, self.sems = part, first, held, second, sems
        self.me, self.parity, self.group, self.partner, self.groups = place(axis, n)
        self.order = list(range(1, self.groups)) + [0]
        self.copies = []

    def peer(self, j):
        return lax.rem(self.group + j, self.groups) * 2 + self.parity

    def start(self):
        self.to_pair = [None] * self.groups
        for j in self.order:
            theirs = lax.rem(self.group + j, self.groups) * 2 + 1 - self.parity
            self.to_pair[j] = remote(
                self.part.at[theirs],
                self.first.at[j],
                self.sems.at[0, j],
                self.sems.at[1, j],
                self.axis,
                self.partner,
            )
            self.to_pair[j].start()
        self.copies += self.to_pair

    def pass_on(self):
        self.to_peer = []
        for j in self.order[:-1]:
            peer = self.peer(j)
            self.to_pair[j].wait_recv()
            self.held[j] = low(wide(self.part[peer]) + wide(self.first[j]))
            copy = remote(
                self.held.at[j],
                self.second.at[j],
                self.sems.at[2, j],
                self.sems.at[3, j],
                self.axis,
                peer,
            )
            copy.start()
            self.to_peer.append(copy)
        self.copies += self.to_peer

    def total(self):
        self.to_pair[0].wait_recv()
        total = wide(self.part[self.me]) + wide(self.first[0])
        for j in self.order[:-1]:
            self.to_peer[j - 1].wait_recv()
            total = total + wide(self.second[j])
        return total

    def drain(self):
        for copy in self.copies:
            copy.wait_send()


class Reduce(Scatter):
    def __init__(self, axis, n, part, first, held, second, whole, sems):
        super().__init__(axis, n, part, first, held, second, sems)
        self.whole = whole

    def gather(self):
        mine = self.whole.at[self.me]
        self.around = []
        for j in range(1, self.groups):
            self.around.append(
                remote(mine, mine, self.sems.at[4, j], self.sems.at[5, j], self.axis, self.peer(j))
            )
            self.around[-1].start()
        across = remote(mine, mine, self.sems.at[6, 0], self.sems.at[7, 0], self.axis, self.partner)
        across.start()
        self.across = [across]

    def forward(self):
        for j in range(1, self.groups):
            self.around[j - 1].wait_recv()
            owner = lax.rem(self.group + self.groups - j, self.groups) * 2 + self.parity
            block = self.whole.at[owner]
            copy = remote(
                block, block, self.sems.at[6, j], self.sems.at[7, j], self.axis, self.partner
            )
            copy.start()
            self.across.append(copy)

    def finish(self):
        for copy in self.across:
            copy.wait_recv()
        self.copies += self.around + self.across


def greet(axes):
    barrier = pltpu.get_barrier_semaphore()
    count = 0
    for axis, n in axes:
        _, parity, group, partner, groups = place(axis, n)
        others = [partner]
        for j in range(1, groups):
            others.append(lax.rem(group + j, groups) * 2 + parity)
        for other in others:
            pl.semaphore_signal(barrier, inc=1, device_id={axis: other}, device_id_type=MESH)
        count += len(others)
    pl.semaphore_wait(barrier, count)


def kernel(
    n,
    m,
    lengths,
    tokens,
    cotangent,
    triple_hbm,
    output_hbm,
    upward_hbm,
    downward_hbm,
    final_hbm,
    triple_out_hbm,
    output_out_hbm,
    upward_out_hbm,
    downward_out_hbm,
    triple_weight,
    output_weight,
    upward_weight,
    downward_weight,
    triple_out,
    output_out,
    upward_out,
    downward_out,
    in_sems,
    out_sems,
    final_sem,
    part,
    first,
    held,
    second,
    whole,
    sems,
    down_part,
    down_first,
    down_held,
    down_second,
    down_sems,
    up_part,
    up_first,
    up_held,
    up_second,
    up_sems,
    att_part,
    att_first,
    att_held,
    att_second,
    att_sems,
    qkv_part,
    qkv_first,
    qkv_held,
    qkv_second,
    qkv_sems,
    normed,
    qkv,
    probs,
    context,
    normed_mid,
    slope,
    activated,
    grad_act,
    grad_preact,
    grad_context,
    grad_qkv,
):
    pairs = (
        (triple_hbm, triple_weight),
        (output_hbm, output_weight),
        (upward_hbm, upward_weight),
        (downward_hbm, downward_weight),
    )
    loads = [
        [pltpu.make_async_copy(far.at[l], near.at[l], in_sems.at[l, i]) for i, (far, near) in enumerate(pairs)]
        for l in range(LAYERS)
    ]
    for layer_loads in loads:
        for copy in layer_loads:
            copy.start()
    greet((("mp", n), ("dp", m)))
    halves, _, chunk, width = tokens.shape
    half_rows = n * chunk
    row_count = halves * half_rows
    slates = row_count // SLATE
    held_cols = output_weight.shape[-1]
    heads = held_cols // HD
    me = lax.axis_index("mp")
    position = lax.broadcasted_iota(jnp.int32, (1, SLATE), 1)

    def rows(ref):
        return ref[...].reshape(row_count, width)

    def half(ref, a):
        return ref[a].reshape(half_rows, width)

    def cut(a):
        return slice(a * half_rows, (a + 1) * half_rows)

    def opened(k, a, value):
        part[k, a] = low(value).reshape(n, chunk, width)
        return reducer(k, a)

    def reducer(k, a):
        refs = [ref.at[k, a] for ref in (part, first, held, second, whole, sems)]
        return Reduce("mp", n, *refs)

    def scatterer(refs, l):
        return Scatter("dp", m, *[ref.at[l] for ref in refs])

    def put_grad(ref, l, value):
        ref[l] = low(value).reshape(m, -1, value.shape[1])

    def slices(s, h):
        block = slice(s * SLATE, (s + 1) * SLATE)
        return block, [slice(i * held_cols + h * HD, i * held_cols + (h + 1) * HD) for i in range(3)]

    def joined(l):
        return jnp.concatenate([triple_weight[l, i] for i in range(3)], axis=-1)

    def nothing():
        return None

    drained = []
    span = range(halves)

    def close(k, steps, own, first_work=nothing, second_work=nothing):
        for step in steps:
            step.pass_on()
        first_work()
        for a in span:
            whole[k, a, me] = low(own(a, steps[a].total()))
            steps[a].gather()
        second_work()
        for step in steps:
            step.forward()
        drained.extend(steps)

    def added(stream):
        return lambda a, total: wide(stream[a, me]) + total

    def normed_back(stream, upstream):
        def own(a, total):
            _, scaled, rscale = normalize(stream[a, me])
            return wide(upstream[a, me]) + norm_backward(scaled, rscale, total)

        return own

    stream = tokens
    arriving = None
    streams, mids = [], []
    for l in range(LAYERS):
        streams.append(stream)
        loads[l][0].wait()
        for a in span:
            if arriving is not None:
                arriving[a].finish()
            normed[l, cut(a)] = normalize(half(stream, a))[0]
            qkv[l, cut(a)] = low(dot(normed[l, cut(a)], joined(l)))
        for s in range(slates):
            live = wide(position < lengths[s])
            for h in range(heads):
                block, (q, k, v) = slices(s, h)
                scores = contract_cols(qkv[l, block, q], qkv[l, block, k]) * HD ** (-0.5)
                weights = jnp.exp(scores) * live
                share = weights / jnp.sum(weights, axis=-1, keepdims=True)
                probs[l, s * heads + h] = share
                context[l, block, h * HD : (h + 1) * HD] = low(dot(low(share), qkv[l, block, v]))
        loads[l][1].wait()
        k_here = 2 * l
        steps = []
        for a in span:
            steps.append(opened(k_here, a, contract_cols(context[l, cut(a)], output_weight[l])))
            steps[a].start()

        def early(l=l):
            loads[l][2].wait()
            loads[l][3].wait()
            if l == LAYERS - 1:
                for a in span:
                    grad_act[cut(a)] = low(dot(half(cotangent, a), downward_weight[l]))

        close(k_here, steps, added(stream), early)
        mid = whole.at[k_here]
        mids.append(mid)
        if l == LAYERS - 1:
            break
        nexts = []
        for a in span:
            steps[a].finish()
            normed_mid[l, cut(a)] = normalize(half(mid, a))[0]
            preact = dot(normed_mid[l, cut(a)], upward_weight[l])
            activated[l, cut(a)] = low(gate(preact))
            nexts.append(
                opened(k_here + 1, a, contract_cols(activated[l, cut(a)], downward_weight[l]))
            )
            nexts[a].start()
            slope[l, cut(a)] = gate_slope(preact)
        close(k_here + 1, nexts, added(mid))
        stream = whole.at[k_here + 1]
        arriving = nexts

    final_k = 2 * LAYERS - 1
    finals = [reducer(final_k, a) for a in span]
    final_copy = pltpu.make_async_copy(whole.at[final_k], final_hbm, final_sem)

    def final_gather():
        for a in span:
            whole[final_k, a, me] = low(wide(mids[-1][a, me]) + finals[a].total())
            finals[a].gather()

    def final_finish():
        for item in finals:
            item.finish()
        final_copy.start()

    def each(name):
        def act():
            for item in finals:
                getattr(item, name)()

        return act

    later = [each("start"), each("pass_on"), final_gather, each("forward"), final_finish]

    def advance():
        if later:
            later.pop(0)()

    stores = [final_copy]

    def store(i, l, near, far):
        copy = pltpu.make_async_copy(near.at[l], far.at[l], out_sems.at[l, i])
        copy.start()
        stores.append(copy)

    def triple_done(scatter, l):
        total = scatter.total()
        for i in range(3):
            triple_out[l, i] = total[:, i * held_cols : (i + 1) * held_cols]
        store(0, l, triple_out, triple_out_hbm)

    def output_done(scatter, l):
        output_out[l] = scatter.total()
        store(1, l, output_out, output_out_hbm)

    def upward_done(scatter, l):
        upward_out[l] = scatter.total()
        store(2, l, upward_out, upward_out_hbm)

    def downward_done(scatter, l):
        downward_out[l] = scatter.total()
        store(3, l, downward_out, downward_out_hbm)

    pending = []

    def flush():
        while pending:
            pending.pop(0)()

    upstream = cotangent
    arriving = steps
    k_next = 2 * LAYERS
    for l in reversed(range(LAYERS)):
        last = l == LAYERS - 1
        steps = []
        for a in span:
            arriving[a].finish()
            if last:
                normed_mid[l, cut(a)] = normalize(half(mids[l], a))[0]
                preact = dot(normed_mid[l, cut(a)], upward_weight[l])
                slope[l, cut(a)] = gate_slope(preact)
                act_back = grad_act[cut(a)]
            else:
                act_back = low(dot(half(upstream, a), downward_weight[l]))
            grad_preact[l, cut(a)] = low(wide(act_back) * slope[l, cut(a)])
            steps.append(
                opened(k_next, a, contract_cols(grad_preact[l, cut(a)], upward_weight[l]))
            )
            steps[a].start()
            if last:
                activated[l, cut(a)] = low(gate(preact))
        down = scatterer((down_part, down_first, down_held, down_second, down_sems), l)
        up = scatterer((up_part, up_first, up_held, up_second, up_sems), l)
        att = scatterer((att_part, att_first, att_held, att_second, att_sems), l)
        triple = scatterer((qkv_part, qkv_first, qkv_held, qkv_second, qkv_sems), l)
        drained += [down, up, att, triple]

        def feed_grads(l=l, down=down, up=up, upstream=upstream):
            put_grad(down_part, l, contract_rows(rows(upstream), activated[l]))
            down.start()
            put_grad(up_part, l, contract_rows(normed_mid[l], grad_preact[l]))
            up.start()

        def feed_pass(l=l, down=down, up=up):
            down.pass_on()
            up.pass_on()
            if l == LAYERS - 1:
                for a in span:
                    opened(final_k, a, contract_cols(activated[l, cut(a)], downward_weight[l]))

        close(k_next, steps, normed_back(mids[l], upstream), feed_grads, feed_pass)
        grad_mid = whole.at[k_next]
        k_next += 1
        for a in span:
            steps[a].finish()
            grad_context[cut(a)] = low(dot(half(grad_mid, a), output_weight[l]))
        advance()
        for s in range(slates):
            for h in range(heads):
                block, (q, k, v) = slices(s, h)
                share = probs[l, s * heads + h]
                back = grad_context[block, h * HD : (h + 1) * HD]
                grad_prob = contract_cols(back, qkv[l, block, v])
                grad_qkv[l, block, v] = low(contract_rows(low(share), back))
                inner = jnp.sum(grad_prob * share, axis=-1, keepdims=True)
                grad_score = low(share * (grad_prob - inner) * HD ** (-0.5))
                grad_qkv[l, block, q] = low(dot(grad_score, qkv[l, block, k]))
                grad_qkv[l, block, k] = low(contract_rows(grad_score, qkv[l, block, q]))

        def att_grad(l=l, grad_mid=grad_mid, att=att):
            put_grad(att_part, l, contract_rows(rows(grad_mid), context[l]))
            att.start()

        def triple_grad(l=l, triple=triple):
            put_grad(qkv_part, l, contract_rows(normed[l], grad_qkv[l]))
            triple.start()

        if l > 0:
            steps = []
            for a in span:
                steps.append(opened(k_next, a, contract_cols(grad_qkv[l, cut(a)], joined(l))))
                steps[a].start()

            def attend_grads(att_grad=att_grad, triple_grad=triple_grad):
                att_grad()
                triple_grad()

            def attend_pass(att=att, triple=triple):
                att.pass_on()
                triple.pass_on()
                advance()

            close(k_next, steps, normed_back(streams[l], grad_mid), attend_grads, attend_pass)
            arriving = steps
            upstream = whole.at[k_next]
            k_next += 1
            pending.append(functools.partial(downward_done, down, l))
            pending.append(functools.partial(upward_done, up, l))
            pending.append(functools.partial(output_done, att, l))
            pending.append(functools.partial(triple_done, triple, l))
        else:
            triple_grad()
            att_grad()
            advance()
            triple.pass_on()
            att.pass_on()
            advance()
            flush()
            downward_done(down, l)
            upward_done(up, l)
            while later:
                advance()
            output_done(att, l)
            triple_done(triple, l)
    drained += finals
    for item in drained:
        item.drain()
    for copy in stores:
        copy.wait()


def hand_over(*refs):
    count = (len(refs) - 1) // 2
    sems = refs[-1]
    copies = [
        pltpu.make_async_copy(refs[i].at[j], refs[count + i].at[j], sems.at[i, j])
        for i in range(count)
        for j in range(refs[i].shape[0])
    ]
    for copy in copies:
        copy.start()
    for copy in copies:
        copy.wait()


def body(
    n, m, tokens, lengths, cotangent, triple_weight, output_weight, upward_weight, downward_weight
):
    row_count, width = tokens.shape
    halves = 2 if (row_count // n) % 32 == 0 else 1
    chunk = row_count // (n * halves)
    share = width // m
    held_cols = output_weight.shape[-1]
    hidden = upward_weight.shape[-1]
    triple_cols = 3 * held_cols
    heads_all = (row_count // SLATE) * (held_cols // HD)
    sums = 2 * LAYERS + 2 * LAYERS - 1
    vmem = pl.BlockSpec(memory_space=pltpu.VMEM)
    smem = pl.BlockSpec(memory_space=pltpu.SMEM)
    anywhere = pl.BlockSpec(memory_space=pl.ANY)
    bf16, f32 = jnp.bfloat16, jnp.float32
    whole = (halves, n, chunk, width)
    weights = (
        triple_weight.transpose(0, 2, 1, 3),
        output_weight,
        upward_weight,
        downward_weight,
    )
    results = [
        jax.ShapeDtypeStruct(whole, bf16),
        jax.ShapeDtypeStruct((LAYERS, 3, share, held_cols), f32),
        jax.ShapeDtypeStruct((LAYERS, share, held_cols), f32),
        jax.ShapeDtypeStruct((LAYERS, share, hidden), f32),
        jax.ShapeDtypeStruct((LAYERS, share, hidden), f32),
    ]

    def grads(columns):
        part = (LAYERS, m, share, columns)
        half = pltpu.VMEM((LAYERS, m // 2, share, columns), bf16)
        return [pltpu.VMEM(part, bf16), half, half, half, pltpu.SemaphoreType.DMA((LAYERS, 4, m // 2))]

    half = pltpu.VMEM((sums, halves, n // 2, chunk, width), bf16)
    full = pltpu.VMEM((sums,) + whole, bf16)
    outs = pl.pallas_call(
        functools.partial(kernel, n, m),
        out_shape=results,
        in_specs=[smem, vmem, vmem] + [anywhere] * 4,
        out_specs=[anywhere] * 5,
        scratch_shapes=[pltpu.VMEM(weight.shape, bf16) for weight in weights]
        + [pltpu.VMEM(result.shape, f32) for result in results[1:]]
        + [
            pltpu.SemaphoreType.DMA((LAYERS, 4)),
            pltpu.SemaphoreType.DMA((LAYERS, 4)),
            pltpu.SemaphoreType.DMA,
        ]
        + [full, half, half, half, full, pltpu.SemaphoreType.DMA((sums, halves, 8, n // 2))]
        + grads(hidden)
        + grads(hidden)
        + grads(held_cols)
        + grads(triple_cols)
        + [
            pltpu.VMEM((LAYERS, row_count, width), bf16),
            pltpu.VMEM((LAYERS, row_count, triple_cols), bf16),
            pltpu.VMEM((LAYERS, heads_all, SLATE, SLATE), f32),
            pltpu.VMEM((LAYERS, row_count, held_cols), bf16),
            pltpu.VMEM((LAYERS, row_count, width), bf16),
            pltpu.VMEM((LAYERS, row_count, hidden), f32),
            pltpu.VMEM((LAYERS, row_count, hidden), bf16),
            pltpu.VMEM((row_count, hidden), bf16),
            pltpu.VMEM((LAYERS, row_count, hidden), bf16),
            pltpu.VMEM((row_count, held_cols), bf16),
            pltpu.VMEM((LAYERS, row_count, triple_cols), bf16),
        ],
        compiler_params=pltpu.CompilerParams(
            collective_id=0, has_side_effects=True, vmem_limit_bytes=60 << 20
        ),
    )(lengths, tokens.reshape(whole), cotangent.reshape(whole), *weights)
    most = max(result.shape[0] for result in results)
    final, triple, output, upward, downward = pl.pallas_call(
        hand_over,
        out_shape=results,
        in_specs=[anywhere] * 5,
        out_specs=[anywhere] * 5,
        scratch_shapes=[pltpu.SemaphoreType.DMA((5, most))],
    )(*outs)
    return (
        final.reshape(row_count, width),
        triple.transpose(0, 2, 1, 3),
        output,
        upward,
        downward,
    )


def solution(mesh):
    placed = (
        P("dp", None),
        P("dp"),
        P("dp", None),
        P(None, None, None, "mp"),
        P(None, None, "mp"),
        P(None, None, "mp"),
        P(None, None, "mp"),
    )
    return jax.shard_map(
        functools.partial(body, mesh.shape["mp"], mesh.shape["dp"]),
        mesh=mesh,
        in_specs=placed,
        out_specs=(
            P("dp", None),
            P(None, "dp", None, "mp"),
            P(None, "dp", "mp"),
            P(None, "dp", "mp"),
            P(None, "dp", "mp"),
        ),
        check_vma=False,
    )
```

```python
import functools

import jax
import jax.numpy as jnp
from jax import lax
from jax.experimental import pallas as pl
from jax.experimental.pallas import tpu as pltpu
from jax.sharding import PartitionSpec as P

HD = 64
SLATE = 256
LAYERS = 2
MESH = pl.DeviceIdType.MESH


epsilon = 1e-06


def normalize(stream):
    widened = stream.astype(jnp.float32)
    rscale = lax.rsqrt(jnp.mean(widened * widened, axis=-1, keepdims=True) + epsilon)
    scaled = widened * rscale
    return (scaled.astype(jnp.bfloat16), scaled, rscale)


def norm_backward(scaled, rscale, upward):
    inner = jnp.mean(upward * scaled, axis=-1, keepdims=True)
    return rscale * (upward - scaled * inner)


def contract_rows(left, right):
    return lax.dot_general(
        left, right, (((0,), (0,)), ((), ())), preferred_element_type=jnp.float32
    )


def contract_cols(left, right):
    return lax.dot_general(
        left, right, (((1,), (1,)), ((), ())), preferred_element_type=jnp.float32
    )


def remote(src, dst, send_sem, recv_sem, axis, device):
    return pltpu.make_async_remote_copy(
        src_ref=src,
        dst_ref=dst,
        send_sem=send_sem,
        recv_sem=recv_sem,
        device_id={axis: device},
        device_id_type=MESH,
    )


def place(axis, n):
    me = lax.axis_index(axis)
    parity = lax.rem(me, 2)
    group = lax.div(me, 2)
    partner = me + 1 - 2 * parity
    groups = n // 2
    return me, parity, group, partner, groups


ROOT = (2.0 / 3.141592653589793) ** 0.5
CUBIC = 0.044715


def gate(preact):
    bent = jnp.tanh(ROOT * (preact + CUBIC * (preact * preact * preact)))
    return 0.5 * preact * (1.0 + bent)


def gate_slope(preact):
    square = preact * preact
    bent = jnp.tanh(ROOT * (preact + CUBIC * (square * preact)))
    inner = ROOT * (1.0 + 3.0 * CUBIC * square)
    return 0.5 * (1.0 + bent) + 0.5 * preact * (1.0 - bent * bent) * inner


def dot(left, right):
    return jnp.dot(left, right, preferred_element_type=jnp.float32)


def low(value):
    return value.astype(jnp.bfloat16)


def wide(value):
    return value.astype(jnp.float32)


class Scatter:
    def __init__(self, axis, n, part, first, held, second, sems):
        self.axis, self.n = axis, n
        self.part, self.first, self.held, self.second, self.sems = part, first, held, second, sems
        self.me, self.parity, self.group, self.partner, self.groups = place(axis, n)
        self.order = list(range(1, self.groups)) + [0]
        self.copies = []

    def peer(self, j):
        return lax.rem(self.group + j, self.groups) * 2 + self.parity

    def start(self):
        self.to_pair = [None] * self.groups
        for j in self.order:
            theirs = lax.rem(self.group + j, self.groups) * 2 + 1 - self.parity
            self.to_pair[j] = remote(
                self.part.at[theirs],
                self.first.at[j],
                self.sems.at[0, j],
                self.sems.at[1, j],
                self.axis,
                self.partner,
            )
            self.to_pair[j].start()
        self.copies += self.to_pair

    def pass_on(self):
        self.to_peer = []
        for j in self.order[:-1]:
            peer = self.peer(j)
            self.to_pair[j].wait_recv()
            self.held[j] = low(wide(self.part[peer]) + wide(self.first[j]))
            copy = remote(
                self.held.at[j],
                self.second.at[j],
                self.sems.at[2, j],
                self.sems.at[3, j],
                self.axis,
                peer,
            )
            copy.start()
            self.to_peer.append(copy)
        self.copies += self.to_peer

    def total(self):
        self.to_pair[0].wait_recv()
        total = wide(self.part[self.me]) + wide(self.first[0])
        for j in self.order[:-1]:
            self.to_peer[j - 1].wait_recv()
            total = total + wide(self.second[j])
        return total

    def drain(self):
        for copy in self.copies:
            copy.wait_send()


class Reduce(Scatter):
    def __init__(self, axis, n, part, first, held, second, whole, sems):
        super().__init__(axis, n, part, first, held, second, sems)
        self.whole = whole

    def gather(self):
        mine = self.whole.at[self.me]
        self.around = []
        for j in range(1, self.groups):
            self.around.append(
                remote(mine, mine, self.sems.at[4, j], self.sems.at[5, j], self.axis, self.peer(j))
            )
            self.around[-1].start()
        across = remote(mine, mine, self.sems.at[6, 0], self.sems.at[7, 0], self.axis, self.partner)
        across.start()
        self.across = [across]

    def forward(self):
        for j in range(1, self.groups):
            self.around[j - 1].wait_recv()
            owner = lax.rem(self.group + self.groups - j, self.groups) * 2 + self.parity
            block = self.whole.at[owner]
            copy = remote(
                block, block, self.sems.at[6, j], self.sems.at[7, j], self.axis, self.partner
            )
            copy.start()
            self.across.append(copy)

    def finish(self):
        for copy in self.across:
            copy.wait_recv()
        self.copies += self.around + self.across


def greet(axes):
    barrier = pltpu.get_barrier_semaphore()
    count = 0
    for axis, n in axes:
        _, parity, group, partner, groups = place(axis, n)
        others = [partner]
        for j in range(1, groups):
            others.append(lax.rem(group + j, groups) * 2 + parity)
        for other in others:
            pl.semaphore_signal(barrier, inc=1, device_id={axis: other}, device_id_type=MESH)
        count += len(others)
    pl.semaphore_wait(barrier, count)


def kernel(
    n,
    m,
    lengths,
    tokens,
    cotangent,
    triple_hbm,
    output_hbm,
    upward_hbm,
    downward_hbm,
    final_hbm,
    triple_out_hbm,
    output_out_hbm,
    upward_out_hbm,
    downward_out_hbm,
    triple_weight,
    output_weight,
    upward_weight,
    downward_weight,
    triple_out,
    output_out,
    upward_out,
    downward_out,
    in_sems,
    out_sems,
    final_sem,
    part,
    first,
    held,
    second,
    whole,
    sems,
    down_part,
    down_first,
    down_held,
    down_second,
    down_sems,
    up_part,
    up_first,
    up_held,
    up_second,
    up_sems,
    att_part,
    att_first,
    att_held,
    att_second,
    att_sems,
    qkv_part,
    qkv_first,
    qkv_held,
    qkv_second,
    qkv_sems,
    normed,
    qkv,
    probs,
    context,
    normed_mid,
    slope,
    activated,
    grad_act,
    grad_preact,
    grad_context,
    grad_qkv,
):
    pairs = (
        (triple_hbm, triple_weight),
        (output_hbm, output_weight),
        (upward_hbm, upward_weight),
        (downward_hbm, downward_weight),
    )
    loads = [
        [pltpu.make_async_copy(far.at[l], near.at[l], in_sems.at[l, i]) for i, (far, near) in enumerate(pairs)]
        for l in range(LAYERS)
    ]
    for layer_loads in loads:
        for copy in layer_loads:
            copy.start()
    greet((("mp", n), ("dp", m)))
    halves, _, chunk, width = tokens.shape
    half_rows = n * chunk
    row_count = halves * half_rows
    slates = row_count // SLATE
    held_cols = output_weight.shape[-1]
    heads = held_cols // HD
    me = lax.axis_index("mp")
    query_rows = min(SLATE, half_rows)
    position = lax.broadcasted_iota(jnp.int32, (1, SLATE), 1)

    def rows(ref):
        return ref[...].reshape(row_count, width)

    def half(ref, a):
        return ref[a].reshape(half_rows, width)

    def cut(a):
        return slice(a * half_rows, (a + 1) * half_rows)

    def opened(k, a, value):
        part[k, a] = low(value).reshape(n, chunk, width)
        return reducer(k, a)

    def reducer(k, a):
        refs = [ref.at[k, a] for ref in (part, first, held, second, whole, sems)]
        return Reduce("mp", n, *refs)

    def scatterer(refs, l):
        return Scatter("dp", m, *[ref.at[l] for ref in refs])

    def grad_work(ref, l, left, right, scatter):
        share = width // m

        def piece(d):
            columns = slice(d * share, (d + 1) * share)
            ref[l, d] = low(contract_rows(left(columns), right()))
            if d == m - 1:
                scatter.start()

        return [functools.partial(piece, d) for d in range(m)]

    def rows_of(ref):
        return lambda columns: ref[:, :, :, columns].reshape(row_count, -1)

    def slices(s, h):
        block = slice(s * SLATE, (s + 1) * SLATE)
        return block, [slice(i * held_cols + h * HD, i * held_cols + (h + 1) * HD) for i in range(3)]

    def joined(l):
        return jnp.concatenate([triple_weight[l, i] for i in range(3)], axis=-1)

    drained = []
    span = range(halves)

    def close(k, steps, own, work=()):
        work = list(work)
        points = 3 * halves
        each = -(-len(work) // points)

        def tick():
            for _ in range(min(each, len(work))):
                work.pop(0)()

        for step in steps:
            tick()
            step.pass_on()
        for a in span:
            tick()
            whole[k, a, me] = low(own(a, steps[a].total()))
            steps[a].gather()
        for step in steps:
            tick()
            step.forward()
        drained.extend(steps)

    def added(stream):
        return lambda a, total: wide(stream[a, me]) + total

    def normed_back(stream, upstream):
        def own(a, total):
            _, scaled, rscale = normalize(stream[a, me])
            return wide(upstream[a, me]) + norm_backward(scaled, rscale, total)

        return own

    stream = tokens
    arriving = None
    streams, mids = [], []
    for l in range(LAYERS):
        streams.append(stream)
        loads[l][0].wait()
        for a in span:
            if arriving is not None:
                arriving[a].finish()
            normed[l, cut(a)] = normalize(half(stream, a))[0]
            qkv[l, cut(a)] = low(dot(normed[l, cut(a)], joined(l)))
        loads[l][1].wait()
        k_here = 2 * l
        steps = []
        for a in span:
            for start in range(a * half_rows, (a + 1) * half_rows, query_rows):
                s, offset = start // SLATE, start % SLATE
                live = wide(position < lengths[s])
                block = slice(start, start + query_rows)
                for h in range(heads):
                    keys, (q, k, v) = slices(s, h)
                    scores = contract_cols(qkv[l, block, q], qkv[l, keys, k]) * HD ** (-0.5)
                    weights = jnp.exp(scores) * live
                    share = weights / jnp.sum(weights, axis=-1, keepdims=True)
                    probs[l, s * heads + h, offset : offset + query_rows] = share
                    context[l, block, h * HD : (h + 1) * HD] = low(
                        dot(low(share), qkv[l, keys, v])
                    )
            steps.append(opened(k_here, a, contract_cols(context[l, cut(a)], output_weight[l])))
            steps[a].start()

        def early(l=l):
            loads[l][2].wait()
            loads[l][3].wait()
            if l == LAYERS - 1:
                for a in span:
                    grad_act[cut(a)] = low(dot(half(cotangent, a), downward_weight[l]))

        close(k_here, steps, added(stream), [early])
        mid = whole.at[k_here]
        mids.append(mid)
        if l == LAYERS - 1:
            break
        nexts = []
        for a in span:
            steps[a].finish()
            normed_mid[l, cut(a)] = normalize(half(mid, a))[0]
            preact = dot(normed_mid[l, cut(a)], upward_weight[l])
            activated[l, cut(a)] = low(gate(preact))
            nexts.append(
                opened(k_here + 1, a, contract_cols(activated[l, cut(a)], downward_weight[l]))
            )
            nexts[a].start()
            slope[l, cut(a)] = gate_slope(preact)
        close(k_here + 1, nexts, added(mid))
        stream = whole.at[k_here + 1]
        arriving = nexts

    final_k = 2 * LAYERS - 1
    finals = [reducer(final_k, a) for a in span]
    final_copy = pltpu.make_async_copy(whole.at[final_k], final_hbm, final_sem)

    def final_gather():
        for a in span:
            whole[final_k, a, me] = low(wide(mids[-1][a, me]) + finals[a].total())
            finals[a].gather()

    def final_finish():
        for item in finals:
            item.finish()
        final_copy.start()

    def each(name):
        def act():
            for item in finals:
                getattr(item, name)()

        return act

    later = [each("start"), each("pass_on"), final_gather, each("forward"), final_finish]

    def advance():
        if later:
            later.pop(0)()

    stores = [final_copy]

    def store(i, l, near, far):
        copy = pltpu.make_async_copy(near.at[l], far.at[l], out_sems.at[l, i])
        copy.start()
        stores.append(copy)

    def triple_done(scatter, l):
        total = scatter.total()
        for i in range(3):
            triple_out[l, i] = total[:, i * held_cols : (i + 1) * held_cols]
        store(0, l, triple_out, triple_out_hbm)

    def output_done(scatter, l):
        output_out[l] = scatter.total()
        store(1, l, output_out, output_out_hbm)

    def upward_done(scatter, l):
        upward_out[l] = scatter.total()
        store(2, l, upward_out, upward_out_hbm)

    def downward_done(scatter, l):
        downward_out[l] = scatter.total()
        store(3, l, downward_out, downward_out_hbm)

    pending = []

    def flush():
        while pending:
            pending.pop(0)()

    upstream = cotangent
    arriving = steps
    k_next = 2 * LAYERS
    for l in reversed(range(LAYERS)):
        last = l == LAYERS - 1
        steps = []
        for a in span:
            arriving[a].finish()
            if last:
                normed_mid[l, cut(a)] = normalize(half(mids[l], a))[0]
                preact = dot(normed_mid[l, cut(a)], upward_weight[l])
                slope[l, cut(a)] = gate_slope(preact)
                act_back = grad_act[cut(a)]
            else:
                act_back = low(dot(half(upstream, a), downward_weight[l]))
            grad_preact[l, cut(a)] = low(wide(act_back) * slope[l, cut(a)])
            steps.append(
                opened(k_next, a, contract_cols(grad_preact[l, cut(a)], upward_weight[l]))
            )
            steps[a].start()
            if last:
                activated[l, cut(a)] = low(gate(preact))
        down = scatterer((down_part, down_first, down_held, down_second, down_sems), l)
        up = scatterer((up_part, up_first, up_held, up_second, up_sems), l)
        att = scatterer((att_part, att_first, att_held, att_second, att_sems), l)
        triple = scatterer((qkv_part, qkv_first, qkv_held, qkv_second, qkv_sems), l)
        drained += [down, up, att, triple]

        def feed_final(a, l=l):
            opened(final_k, a, contract_cols(activated[l, cut(a)], downward_weight[l]))

        work = grad_work(down_part, l, rows_of(upstream), lambda l=l: activated[l], down)
        work += grad_work(
            up_part, l, lambda c, l=l: normed_mid[l, :, c], lambda l=l: grad_preact[l], up
        )
        work.append(down.pass_on)
        if last:
            work += [functools.partial(feed_final, a) for a in span]
        close(k_next, steps, normed_back(mids[l], upstream), work)
        grad_mid = whole.at[k_next]
        k_next += 1
        for a in span:
            steps[a].finish()
            grad_context[cut(a)] = low(dot(half(grad_mid, a), output_weight[l]))
        up.pass_on()
        advance()
        for s in range(slates):
            for h in range(heads):
                block, (q, k, v) = slices(s, h)
                share = probs[l, s * heads + h]
                back = grad_context[block, h * HD : (h + 1) * HD]
                grad_prob = contract_cols(back, qkv[l, block, v])
                grad_qkv[l, block, v] = low(contract_rows(low(share), back))
                inner = jnp.sum(grad_prob * share, axis=-1, keepdims=True)
                grad_score = low(share * (grad_prob - inner) * HD ** (-0.5))
                grad_qkv[l, block, q] = low(dot(grad_score, qkv[l, block, k]))
                grad_qkv[l, block, k] = low(contract_rows(grad_score, qkv[l, block, q]))

        att_work = grad_work(
            att_part, l, rows_of(grad_mid), lambda l=l: context[l], att
        )
        triple_work = grad_work(
            qkv_part, l, lambda c, l=l: normed[l, :, c], lambda l=l: grad_qkv[l], triple
        )
        if l > 0:
            steps = []
            for a in span:
                steps.append(opened(k_next, a, contract_cols(grad_qkv[l, cut(a)], joined(l))))
                steps[a].start()
            work = triple_work + att_work + [advance, triple.pass_on, att.pass_on]
            close(k_next, steps, normed_back(streams[l], grad_mid), work)
            arriving = steps
            upstream = whole.at[k_next]
            k_next += 1
            pending.append(functools.partial(downward_done, down, l))
            pending.append(functools.partial(upward_done, up, l))
            pending.append(functools.partial(output_done, att, l))
            pending.append(functools.partial(triple_done, triple, l))
        else:
            for item in triple_work + att_work:
                item()
            advance()
            triple.pass_on()
            att.pass_on()
            advance()
            flush()
            downward_done(down, l)
            upward_done(up, l)
            while later:
                advance()
            output_done(att, l)
            triple_done(triple, l)
    drained += finals
    for item in drained:
        item.drain()
    for copy in stores:
        copy.wait()


def hand_over(*refs):
    count = (len(refs) - 1) // 3
    sources, targets, staged, sems = refs[:count], refs[count : 2 * count], refs[2 * count : -1], refs[-1]
    pairs = [(i, j) for i in range(count) for j in range(sources[i].shape[0])]
    ins = [pltpu.make_async_copy(sources[i].at[j], staged[i].at[j], sems.at[0, i, j]) for i, j in pairs]
    outs = [pltpu.make_async_copy(staged[i].at[j], targets[i].at[j], sems.at[1, i, j]) for i, j in pairs]
    for copy in ins:
        copy.start()
    for copy, onward in zip(ins, outs):
        copy.wait()
        onward.start()
    for copy in outs:
        copy.wait()


def body(
    n, m, tokens, lengths, cotangent, triple_weight, output_weight, upward_weight, downward_weight
):
    row_count, width = tokens.shape
    halves = 2 if (row_count // n) % 32 == 0 else 1
    chunk = row_count // (n * halves)
    share = width // m
    held_cols = output_weight.shape[-1]
    hidden = upward_weight.shape[-1]
    triple_cols = 3 * held_cols
    heads_all = (row_count // SLATE) * (held_cols // HD)
    sums = 2 * LAYERS + 2 * LAYERS - 1
    vmem = pl.BlockSpec(memory_space=pltpu.VMEM)
    smem = pl.BlockSpec(memory_space=pltpu.SMEM)
    anywhere = pl.BlockSpec(memory_space=pl.ANY)
    bf16, f32 = jnp.bfloat16, jnp.float32
    whole = (halves, n, chunk, width)
    weights = (
        triple_weight.transpose(0, 2, 1, 3),
        output_weight,
        upward_weight,
        downward_weight,
    )
    results = [
        jax.ShapeDtypeStruct(whole, bf16),
        jax.ShapeDtypeStruct((LAYERS, 3, share, held_cols), f32),
        jax.ShapeDtypeStruct((LAYERS, share, held_cols), f32),
        jax.ShapeDtypeStruct((LAYERS, share, hidden), f32),
        jax.ShapeDtypeStruct((LAYERS, share, hidden), f32),
    ]

    def grads(columns):
        part = (LAYERS, m, share, columns)
        half = pltpu.VMEM((LAYERS, m // 2, share, columns), bf16)
        return [pltpu.VMEM(part, bf16), half, half, half, pltpu.SemaphoreType.DMA((LAYERS, 4, m // 2))]

    half = pltpu.VMEM((sums, halves, n // 2, chunk, width), bf16)
    full = pltpu.VMEM((sums,) + whole, bf16)
    outs = pl.pallas_call(
        functools.partial(kernel, n, m),
        out_shape=results,
        in_specs=[smem, vmem, vmem] + [anywhere] * 4,
        out_specs=[anywhere] * 5,
        scratch_shapes=[pltpu.VMEM(weight.shape, bf16) for weight in weights]
        + [pltpu.VMEM(result.shape, f32) for result in results[1:]]
        + [
            pltpu.SemaphoreType.DMA((LAYERS, 4)),
            pltpu.SemaphoreType.DMA((LAYERS, 4)),
            pltpu.SemaphoreType.DMA,
        ]
        + [full, half, half, half, full, pltpu.SemaphoreType.DMA((sums, halves, 8, n // 2))]
        + grads(hidden)
        + grads(hidden)
        + grads(held_cols)
        + grads(triple_cols)
        + [
            pltpu.VMEM((LAYERS, row_count, width), bf16),
            pltpu.VMEM((LAYERS, row_count, triple_cols), bf16),
            pltpu.VMEM((LAYERS, heads_all, SLATE, SLATE), f32),
            pltpu.VMEM((LAYERS, row_count, held_cols), bf16),
            pltpu.VMEM((LAYERS, row_count, width), bf16),
            pltpu.VMEM((LAYERS, row_count, hidden), f32),
            pltpu.VMEM((LAYERS, row_count, hidden), bf16),
            pltpu.VMEM((row_count, hidden), bf16),
            pltpu.VMEM((LAYERS, row_count, hidden), bf16),
            pltpu.VMEM((row_count, held_cols), bf16),
            pltpu.VMEM((LAYERS, row_count, triple_cols), bf16),
        ],
        compiler_params=pltpu.CompilerParams(
            collective_id=0, has_side_effects=True, vmem_limit_bytes=60 << 20
        ),
    )(lengths, tokens.reshape(whole), cotangent.reshape(whole), *weights)
    most = max(result.shape[0] for result in results)
    final, triple, output, upward, downward = pl.pallas_call(
        hand_over,
        out_shape=results,
        in_specs=[anywhere] * 5,
        out_specs=[anywhere] * 5,
        scratch_shapes=[pltpu.VMEM(result.shape, result.dtype) for result in results]
        + [pltpu.SemaphoreType.DMA((2, 5, most))],
        compiler_params=pltpu.CompilerParams(vmem_limit_bytes=16 << 20),
    )(*outs)
    return (
        final.reshape(row_count, width),
        triple.transpose(0, 2, 1, 3),
        output,
        upward,
        downward,
    )


def solution(mesh):
    placed = (
        P("dp", None),
        P("dp"),
        P("dp", None),
        P(None, None, None, "mp"),
        P(None, None, "mp"),
        P(None, None, "mp"),
        P(None, None, "mp"),
    )
    return jax.shard_map(
        functools.partial(body, mesh.shape["mp"], mesh.shape["dp"]),
        mesh=mesh,
        in_specs=placed,
        out_specs=(
            P("dp", None),
            P(None, "dp", None, "mp"),
            P(None, "dp", "mp"),
            P(None, "dp", "mp"),
            P(None, "dp", "mp"),
        ),
        check_vma=False,
    )
```

```python
import functools

import jax
import jax.numpy as jnp
from jax import lax
from jax.experimental import pallas as pl
from jax.experimental.pallas import tpu as pltpu
from jax.sharding import PartitionSpec as P

HD = 64
SLATE = 256
LAYERS = 2
MESH = pl.DeviceIdType.MESH


epsilon = 1e-06


def normalize(stream):
    widened = stream.astype(jnp.float32)
    rscale = lax.rsqrt(jnp.mean(widened * widened, axis=-1, keepdims=True) + epsilon)
    scaled = widened * rscale
    return (scaled.astype(jnp.bfloat16), scaled, rscale)


def norm_backward(scaled, rscale, upward):
    inner = jnp.mean(upward * scaled, axis=-1, keepdims=True)
    return rscale * (upward - scaled * inner)


def contract_rows(left, right):
    return lax.dot_general(
        left, right, (((0,), (0,)), ((), ())), preferred_element_type=jnp.float32
    )


def contract_cols(left, right):
    return lax.dot_general(
        left, right, (((1,), (1,)), ((), ())), preferred_element_type=jnp.float32
    )


def remote(src, dst, send_sem, recv_sem, axis, device):
    return pltpu.make_async_remote_copy(
        src_ref=src,
        dst_ref=dst,
        send_sem=send_sem,
        recv_sem=recv_sem,
        device_id={axis: device},
        device_id_type=MESH,
    )


def place(axis, n):
    me = lax.axis_index(axis)
    parity = lax.rem(me, 2)
    group = lax.div(me, 2)
    partner = me + 1 - 2 * parity
    groups = n // 2
    return me, parity, group, partner, groups


ROOT = (2.0 / 3.141592653589793) ** 0.5
CUBIC = 0.044715


def gate(preact):
    bent = jnp.tanh(ROOT * (preact + CUBIC * (preact * preact * preact)))
    return 0.5 * preact * (1.0 + bent)


def gate_slope(preact):
    square = preact * preact
    bent = jnp.tanh(ROOT * (preact + CUBIC * (square * preact)))
    inner = ROOT * (1.0 + 3.0 * CUBIC * square)
    return 0.5 * (1.0 + bent) + 0.5 * preact * (1.0 - bent * bent) * inner


def dot(left, right):
    return jnp.dot(left, right, preferred_element_type=jnp.float32)


def low(value):
    return value.astype(jnp.bfloat16)


def wide(value):
    return value.astype(jnp.float32)


class Scatter:
    def __init__(self, axis, n, part, first, held, second, sems):
        self.axis, self.n = axis, n
        self.part, self.first, self.held, self.second, self.sems = part, first, held, second, sems
        self.me, self.parity, self.group, self.partner, self.groups = place(axis, n)
        self.order = list(range(1, self.groups)) + [0]
        self.copies = []

    def peer(self, j):
        return lax.rem(self.group + j, self.groups) * 2 + self.parity

    def start(self):
        self.to_pair = [None] * self.groups
        for j in self.order:
            theirs = lax.rem(self.group + j, self.groups) * 2 + 1 - self.parity
            self.to_pair[j] = remote(
                self.part.at[theirs],
                self.first.at[j],
                self.sems.at[0, j],
                self.sems.at[1, j],
                self.axis,
                self.partner,
            )
            self.to_pair[j].start()
        self.copies += self.to_pair

    def pass_on(self):
        self.to_peer = []
        for j in self.order[:-1]:
            peer = self.peer(j)
            self.to_pair[j].wait_recv()
            self.held[j] = low(wide(self.part[peer]) + wide(self.first[j]))
            copy = remote(
                self.held.at[j],
                self.second.at[j],
                self.sems.at[2, j],
                self.sems.at[3, j],
                self.axis,
                peer,
            )
            copy.start()
            self.to_peer.append(copy)
        self.copies += self.to_peer

    def total(self):
        self.to_pair[0].wait_recv()
        total = wide(self.part[self.me]) + wide(self.first[0])
        for j in self.order[:-1]:
            self.to_peer[j - 1].wait_recv()
            total = total + wide(self.second[j])
        return total

    def drain(self):
        for copy in self.copies:
            copy.wait_send()


class Reduce(Scatter):
    def __init__(self, axis, n, part, first, held, second, whole, sems):
        super().__init__(axis, n, part, first, held, second, sems)
        self.whole = whole

    def gather(self):
        mine = self.whole.at[self.me]
        self.around = []
        for j in range(1, self.groups):
            self.around.append(
                remote(mine, mine, self.sems.at[4, j], self.sems.at[5, j], self.axis, self.peer(j))
            )
            self.around[-1].start()
        across = remote(mine, mine, self.sems.at[6, 0], self.sems.at[7, 0], self.axis, self.partner)
        across.start()
        self.across = [across]

    def forward(self):
        for j in range(1, self.groups):
            self.around[j - 1].wait_recv()
            owner = lax.rem(self.group + self.groups - j, self.groups) * 2 + self.parity
            block = self.whole.at[owner]
            copy = remote(
                block, block, self.sems.at[6, j], self.sems.at[7, j], self.axis, self.partner
            )
            copy.start()
            self.across.append(copy)

    def finish(self):
        for copy in self.across:
            copy.wait_recv()
        self.copies += self.around + self.across


def greet(axes):
    barrier = pltpu.get_barrier_semaphore()
    count = 0
    for axis, n in axes:
        _, parity, group, partner, groups = place(axis, n)
        others = [partner]
        for j in range(1, groups):
            others.append(lax.rem(group + j, groups) * 2 + parity)
        for other in others:
            pl.semaphore_signal(barrier, inc=1, device_id={axis: other}, device_id_type=MESH)
        count += len(others)
    return count


def kernel(
    n,
    m,
    lengths,
    tokens,
    cotangent,
    triple_hbm,
    output_hbm,
    upward_hbm,
    downward_hbm,
    final_hbm,
    triple_out_hbm,
    output_out_hbm,
    upward_out_hbm,
    downward_out_hbm,
    triple_weight,
    output_weight,
    upward_weight,
    downward_weight,
    triple_out,
    output_out,
    upward_out,
    downward_out,
    in_sems,
    out_sems,
    final_sem,
    part,
    first,
    held,
    second,
    whole,
    sems,
    down_part,
    down_first,
    down_held,
    down_second,
    down_sems,
    up_part,
    up_first,
    up_held,
    up_second,
    up_sems,
    att_part,
    att_first,
    att_held,
    att_second,
    att_sems,
    qkv_part,
    qkv_first,
    qkv_held,
    qkv_second,
    qkv_sems,
    normed,
    qkv,
    probs,
    context,
    normed_mid,
    slope,
    activated,
    grad_act,
    grad_preact,
    grad_context,
    grad_qkv,
):
    pairs = (
        (triple_hbm, triple_weight),
        (output_hbm, output_weight),
        (upward_hbm, upward_weight),
        (downward_hbm, downward_weight),
    )
    loads = [
        [pltpu.make_async_copy(far.at[l], near.at[l], in_sems.at[l, i]) for i, (far, near) in enumerate(pairs)]
        for l in range(LAYERS)
    ]
    for layer_loads in loads:
        for copy in layer_loads:
            copy.start()
    greeted = greet((("mp", n), ("dp", m)))
    halves, _, chunk, width = tokens.shape
    half_rows = n * chunk
    row_count = halves * half_rows
    slates = row_count // SLATE
    held_cols = output_weight.shape[-1]
    heads = held_cols // HD
    me = lax.axis_index("mp")
    query_rows = min(SLATE, half_rows)
    position = lax.broadcasted_iota(jnp.int32, (1, SLATE), 1)

    def rows(ref):
        return ref[...].reshape(row_count, width)

    def half(ref, a):
        return ref[a].reshape(half_rows, width)

    def cut(a):
        return slice(a * half_rows, (a + 1) * half_rows)

    def opened(k, a, value):
        part[k, a] = low(value).reshape(n, chunk, width)
        return reducer(k, a)

    def reducer(k, a):
        refs = [ref.at[k, a] for ref in (part, first, held, second, whole, sems)]
        return Reduce("mp", n, *refs)

    def scatterer(refs, l):
        return Scatter("dp", m, *[ref.at[l] for ref in refs])

    def grad_work(ref, l, left, right, scatter):
        share = width // m

        def piece(d):
            columns = slice(d * share, (d + 1) * share)
            ref[l, d] = low(contract_rows(left(columns), right()))
            if d == m - 1:
                scatter.start()

        return [functools.partial(piece, d) for d in range(m)]

    def rows_of(ref):
        return lambda columns: ref[:, :, :, columns].reshape(row_count, -1)

    def slices(s, h):
        block = slice(s * SLATE, (s + 1) * SLATE)
        return block, [slice(i * held_cols + h * HD, i * held_cols + (h + 1) * HD) for i in range(3)]

    def joined(l):
        return jnp.concatenate([triple_weight[l, i] for i in range(3)], axis=-1)

    drained = []
    span = range(halves)

    def close(k, steps, own, work=()):
        work = list(work)
        each = -(-len(work) // (2 * halves - 1))

        def tick():
            for _ in range(min(each, len(work))):
                work.pop(0)()

        for step in steps:
            step.pass_on()
        for a in span:
            if a > 0:
                tick()
            whole[k, a, me] = low(own(a, steps[a].total()))
            steps[a].gather()
        for step in steps:
            tick()
            step.forward()
        drained.extend(steps)

    def added(stream):
        return lambda a, total: wide(stream[a, me]) + total

    def normed_back(stream, upstream):
        def own(a, total):
            _, scaled, rscale = normalize(stream[a, me])
            return wide(upstream[a, me]) + norm_backward(scaled, rscale, total)

        return own

    stream = tokens
    arriving = None
    streams, mids = [], []
    for l in range(LAYERS):
        streams.append(stream)
        loads[l][0].wait()
        for a in span:
            if arriving is not None:
                arriving[a].finish()
            normed[l, cut(a)] = normalize(half(stream, a))[0]
            qkv[l, cut(a)] = low(dot(normed[l, cut(a)], joined(l)))
        loads[l][1].wait()
        k_here = 2 * l
        steps = []
        for a in span:
            for start in range(a * half_rows, (a + 1) * half_rows, query_rows):
                s, offset = start // SLATE, start % SLATE
                live = wide(position < lengths[s])
                block = slice(start, start + query_rows)
                for h in range(heads):
                    keys, (q, k, v) = slices(s, h)
                    scores = contract_cols(qkv[l, block, q], qkv[l, keys, k]) * HD ** (-0.5)
                    weights = jnp.exp(scores) * live
                    share = weights / jnp.sum(weights, axis=-1, keepdims=True)
                    probs[l, s * heads + h, offset : offset + query_rows] = share
                    context[l, block, h * HD : (h + 1) * HD] = low(
                        dot(low(share), qkv[l, keys, v])
                    )
            steps.append(opened(k_here, a, contract_cols(context[l, cut(a)], output_weight[l])))
            if l == 0 and a == 0:
                pl.semaphore_wait(pltpu.get_barrier_semaphore(), greeted)
            steps[a].start()

        def early(l=l):
            loads[l][2].wait()
            loads[l][3].wait()
            if l == LAYERS - 1:
                for a in span:
                    grad_act[cut(a)] = low(dot(half(cotangent, a), downward_weight[l]))

        close(k_here, steps, added(stream), [early])
        mid = whole.at[k_here]
        mids.append(mid)
        if l == LAYERS - 1:
            break
        nexts = []
        for a in span:
            steps[a].finish()
            normed_mid[l, cut(a)] = normalize(half(mid, a))[0]
            preact = dot(normed_mid[l, cut(a)], upward_weight[l])
            activated[l, cut(a)] = low(gate(preact))
            nexts.append(
                opened(k_here + 1, a, contract_cols(activated[l, cut(a)], downward_weight[l]))
            )
            nexts[a].start()
            slope[l, cut(a)] = gate_slope(preact)
        close(k_here + 1, nexts, added(mid))
        stream = whole.at[k_here + 1]
        arriving = nexts

    final_k = 2 * LAYERS - 1
    finals = [reducer(final_k, a) for a in span]
    final_copy = pltpu.make_async_copy(whole.at[final_k], final_hbm, final_sem)

    def final_gather():
        for a in span:
            whole[final_k, a, me] = low(wide(mids[-1][a, me]) + finals[a].total())
            finals[a].gather()

    def final_finish():
        for item in finals:
            item.finish()
        final_copy.start()

    def each(name):
        def act():
            for item in finals:
                getattr(item, name)()

        return act

    later = [each("start"), each("pass_on"), final_gather, each("forward"), final_finish]

    def advance():
        if later:
            later.pop(0)()

    stores = [final_copy]

    def store(i, l, near, far):
        copy = pltpu.make_async_copy(near.at[l], far.at[l], out_sems.at[l, i])
        copy.start()
        stores.append(copy)

    def triple_done(scatter, l):
        total = scatter.total()
        for i in range(3):
            triple_out[l, i] = total[:, i * held_cols : (i + 1) * held_cols]
        store(0, l, triple_out, triple_out_hbm)

    def output_done(scatter, l):
        output_out[l] = scatter.total()
        store(1, l, output_out, output_out_hbm)

    def upward_done(scatter, l):
        upward_out[l] = scatter.total()
        store(2, l, upward_out, upward_out_hbm)

    def downward_done(scatter, l):
        downward_out[l] = scatter.total()
        store(3, l, downward_out, downward_out_hbm)

    pending = []

    def flush():
        while pending:
            pending.pop(0)()

    upstream = cotangent
    arriving = steps
    k_next = 2 * LAYERS
    for l in reversed(range(LAYERS)):
        last = l == LAYERS - 1
        steps = []
        for a in span:
            arriving[a].finish()
            if last:
                normed_mid[l, cut(a)] = normalize(half(mids[l], a))[0]
                preact = dot(normed_mid[l, cut(a)], upward_weight[l])
                slope[l, cut(a)] = gate_slope(preact)
                act_back = grad_act[cut(a)]
            else:
                act_back = low(dot(half(upstream, a), downward_weight[l]))
            grad_preact[l, cut(a)] = low(wide(act_back) * slope[l, cut(a)])
            steps.append(
                opened(k_next, a, contract_cols(grad_preact[l, cut(a)], upward_weight[l]))
            )
            steps[a].start()
            if last:
                activated[l, cut(a)] = low(gate(preact))
        down = scatterer((down_part, down_first, down_held, down_second, down_sems), l)
        up = scatterer((up_part, up_first, up_held, up_second, up_sems), l)
        att = scatterer((att_part, att_first, att_held, att_second, att_sems), l)
        triple = scatterer((qkv_part, qkv_first, qkv_held, qkv_second, qkv_sems), l)
        drained += [down, up, att, triple]

        def feed_final(a, l=l):
            opened(final_k, a, contract_cols(activated[l, cut(a)], downward_weight[l]))

        work = grad_work(down_part, l, rows_of(upstream), lambda l=l: activated[l], down)
        work += grad_work(
            up_part, l, lambda c, l=l: normed_mid[l, :, c], lambda l=l: grad_preact[l], up
        )
        work.append(down.pass_on)
        if last:
            work += [functools.partial(feed_final, a) for a in span]
        close(k_next, steps, normed_back(mids[l], upstream), work)
        grad_mid = whole.at[k_next]
        k_next += 1
        for a in span:
            steps[a].finish()
            grad_context[cut(a)] = low(dot(half(grad_mid, a), output_weight[l]))
        up.pass_on()
        advance()
        for s in range(slates):
            for h in range(heads):
                block, (q, k, v) = slices(s, h)
                share = probs[l, s * heads + h]
                back = grad_context[block, h * HD : (h + 1) * HD]
                grad_prob = contract_cols(back, qkv[l, block, v])
                grad_qkv[l, block, v] = low(contract_rows(low(share), back))
                inner = jnp.sum(grad_prob * share, axis=-1, keepdims=True)
                grad_score = low(share * (grad_prob - inner) * HD ** (-0.5))
                grad_qkv[l, block, q] = low(dot(grad_score, qkv[l, block, k]))
                grad_qkv[l, block, k] = low(contract_rows(grad_score, qkv[l, block, q]))

        att_work = grad_work(
            att_part, l, rows_of(grad_mid), lambda l=l: context[l], att
        )
        triple_work = grad_work(
            qkv_part, l, lambda c, l=l: normed[l, :, c], lambda l=l: grad_qkv[l], triple
        )
        if l > 0:
            steps = []
            for a in span:
                steps.append(opened(k_next, a, contract_cols(grad_qkv[l, cut(a)], joined(l))))
                steps[a].start()
            work = triple_work + att_work + [advance, triple.pass_on, att.pass_on]
            close(k_next, steps, normed_back(streams[l], grad_mid), work)
            arriving = steps
            upstream = whole.at[k_next]
            k_next += 1
            pending.append(functools.partial(downward_done, down, l))
            pending.append(functools.partial(upward_done, up, l))
            pending.append(functools.partial(output_done, att, l))
            pending.append(functools.partial(triple_done, triple, l))
        else:
            for item in triple_work + att_work:
                item()
            advance()
            triple.pass_on()
            att.pass_on()
            advance()
            flush()
            downward_done(down, l)
            upward_done(up, l)
            while later:
                advance()
            output_done(att, l)
            triple_done(triple, l)
    drained += finals
    for item in drained:
        item.drain()
    for copy in stores:
        copy.wait()


def hand_over(*refs):
    count = (len(refs) - 1) // 3
    sources, targets, staged, sems = refs[:count], refs[count : 2 * count], refs[2 * count : -1], refs[-1]
    pairs = [(i, j) for i in range(count) for j in range(sources[i].shape[0])]
    ins = [pltpu.make_async_copy(sources[i].at[j], staged[i].at[j], sems.at[0, i, j]) for i, j in pairs]
    outs = [pltpu.make_async_copy(staged[i].at[j], targets[i].at[j], sems.at[1, i, j]) for i, j in pairs]
    for copy in ins:
        copy.start()
    for copy, onward in zip(ins, outs):
        copy.wait()
        onward.start()
    for copy in outs:
        copy.wait()


def body(
    n, m, tokens, lengths, cotangent, triple_weight, output_weight, upward_weight, downward_weight
):
    row_count, width = tokens.shape
    halves = 2 if (row_count // n) % 32 == 0 else 1
    chunk = row_count // (n * halves)
    share = width // m
    held_cols = output_weight.shape[-1]
    hidden = upward_weight.shape[-1]
    triple_cols = 3 * held_cols
    heads_all = (row_count // SLATE) * (held_cols // HD)
    sums = 2 * LAYERS + 2 * LAYERS - 1
    vmem = pl.BlockSpec(memory_space=pltpu.VMEM)
    smem = pl.BlockSpec(memory_space=pltpu.SMEM)
    anywhere = pl.BlockSpec(memory_space=pl.ANY)
    bf16, f32 = jnp.bfloat16, jnp.float32
    whole = (halves, n, chunk, width)
    weights = (
        triple_weight.transpose(0, 2, 1, 3),
        output_weight,
        upward_weight,
        downward_weight,
    )
    results = [
        jax.ShapeDtypeStruct(whole, bf16),
        jax.ShapeDtypeStruct((LAYERS, 3, share, held_cols), f32),
        jax.ShapeDtypeStruct((LAYERS, share, held_cols), f32),
        jax.ShapeDtypeStruct((LAYERS, share, hidden), f32),
        jax.ShapeDtypeStruct((LAYERS, share, hidden), f32),
    ]

    def grads(columns):
        part = (LAYERS, m, share, columns)
        half = pltpu.VMEM((LAYERS, m // 2, share, columns), bf16)
        return [pltpu.VMEM(part, bf16), half, half, half, pltpu.SemaphoreType.DMA((LAYERS, 4, m // 2))]

    half = pltpu.VMEM((sums, halves, n // 2, chunk, width), bf16)
    full = pltpu.VMEM((sums,) + whole, bf16)
    outs = pl.pallas_call(
        functools.partial(kernel, n, m),
        out_shape=results,
        in_specs=[smem, vmem, vmem] + [anywhere] * 4,
        out_specs=[anywhere] * 5,
        scratch_shapes=[pltpu.VMEM(weight.shape, bf16) for weight in weights]
        + [pltpu.VMEM(result.shape, f32) for result in results[1:]]
        + [
            pltpu.SemaphoreType.DMA((LAYERS, 4)),
            pltpu.SemaphoreType.DMA((LAYERS, 4)),
            pltpu.SemaphoreType.DMA,
        ]
        + [full, half, half, half, full, pltpu.SemaphoreType.DMA((sums, halves, 8, n // 2))]
        + grads(hidden)
        + grads(hidden)
        + grads(held_cols)
        + grads(triple_cols)
        + [
            pltpu.VMEM((LAYERS, row_count, width), bf16),
            pltpu.VMEM((LAYERS, row_count, triple_cols), bf16),
            pltpu.VMEM((LAYERS, heads_all, SLATE, SLATE), f32),
            pltpu.VMEM((LAYERS, row_count, held_cols), bf16),
            pltpu.VMEM((LAYERS, row_count, width), bf16),
            pltpu.VMEM((LAYERS, row_count, hidden), f32),
            pltpu.VMEM((LAYERS, row_count, hidden), bf16),
            pltpu.VMEM((row_count, hidden), bf16),
            pltpu.VMEM((LAYERS, row_count, hidden), bf16),
            pltpu.VMEM((row_count, held_cols), bf16),
            pltpu.VMEM((LAYERS, row_count, triple_cols), bf16),
        ],
        compiler_params=pltpu.CompilerParams(
            collective_id=0, has_side_effects=True, vmem_limit_bytes=60 << 20
        ),
    )(lengths, tokens.reshape(whole), cotangent.reshape(whole), *weights)
    most = max(result.shape[0] for result in results)
    final, triple, output, upward, downward = pl.pallas_call(
        hand_over,
        out_shape=results,
        in_specs=[anywhere] * 5,
        out_specs=[anywhere] * 5,
        scratch_shapes=[pltpu.VMEM(result.shape, result.dtype) for result in results]
        + [pltpu.SemaphoreType.DMA((2, 5, most))],
    )(*outs)
    return (
        final.reshape(row_count, width),
        triple.transpose(0, 2, 1, 3),
        output,
        upward,
        downward,
    )


def solution(mesh):
    placed = (
        P("dp", None),
        P("dp"),
        P("dp", None),
        P(None, None, None, "mp"),
        P(None, None, "mp"),
        P(None, None, "mp"),
        P(None, None, "mp"),
    )
    return jax.shard_map(
        functools.partial(body, mesh.shape["mp"], mesh.shape["dp"]),
        mesh=mesh,
        in_specs=placed,
        out_specs=(
            P("dp", None),
            P(None, "dp", None, "mp"),
            P(None, "dp", "mp"),
            P(None, "dp", "mp"),
            P(None, "dp", "mp"),
        ),
        check_vma=False,
    )
```

```python
import functools

import jax
import jax.numpy as jnp
from jax import lax
from jax.experimental import pallas as pl
from jax.experimental.pallas import tpu as pltpu
from jax.sharding import PartitionSpec as P

HD = 64
SLATE = 256
LAYERS = 2
MESH = pl.DeviceIdType.MESH


epsilon = 1e-06


def normalize(stream):
    widened = stream.astype(jnp.float32)
    rscale = lax.rsqrt(jnp.mean(widened * widened, axis=-1, keepdims=True) + epsilon)
    scaled = widened * rscale
    return (scaled.astype(jnp.bfloat16), scaled, rscale)


def norm_backward(scaled, rscale, upward):
    inner = jnp.mean(upward * scaled, axis=-1, keepdims=True)
    return rscale * (upward - scaled * inner)


def contract_rows(left, right):
    return lax.dot_general(
        left, right, (((0,), (0,)), ((), ())), preferred_element_type=jnp.float32
    )


def contract_cols(left, right):
    return lax.dot_general(
        left, right, (((1,), (1,)), ((), ())), preferred_element_type=jnp.float32
    )


def remote(src, dst, send_sem, recv_sem, axis, device):
    return pltpu.make_async_remote_copy(
        src_ref=src,
        dst_ref=dst,
        send_sem=send_sem,
        recv_sem=recv_sem,
        device_id={axis: device},
        device_id_type=MESH,
    )


def place(axis, n):
    me = lax.axis_index(axis)
    parity = lax.rem(me, 2)
    group = lax.div(me, 2)
    partner = me + 1 - 2 * parity
    groups = n // 2
    return me, parity, group, partner, groups


ROOT = (2.0 / 3.141592653589793) ** 0.5
CUBIC = 0.044715


def gate(preact):
    bent = jnp.tanh(ROOT * (preact + CUBIC * (preact * preact * preact)))
    return 0.5 * preact * (1.0 + bent)


def gate_slope(preact):
    square = preact * preact
    bent = jnp.tanh(ROOT * (preact + CUBIC * (square * preact)))
    inner = ROOT * (1.0 + 3.0 * CUBIC * square)
    return 0.5 * (1.0 + bent) + 0.5 * preact * (1.0 - bent * bent) * inner


def dot(left, right):
    return jnp.dot(left, right, preferred_element_type=jnp.float32)


def low(value):
    return value.astype(jnp.bfloat16)


def wide(value):
    return value.astype(jnp.float32)


class Scatter:
    def __init__(self, axis, n, part, first, held, second, sems):
        self.axis, self.n = axis, n
        self.part, self.first, self.held, self.second, self.sems = part, first, held, second, sems
        self.me, self.parity, self.group, self.partner, self.groups = place(axis, n)
        self.order = list(range(1, self.groups)) + [0]
        self.copies = []

    def peer(self, j):
        return lax.rem(self.group + j, self.groups) * 2 + self.parity

    def start(self):
        self.to_pair = [None] * self.groups
        for j in self.order:
            theirs = lax.rem(self.group + j, self.groups) * 2 + 1 - self.parity
            self.to_pair[j] = remote(
                self.part.at[theirs],
                self.first.at[j],
                self.sems.at[0, j],
                self.sems.at[1, j],
                self.axis,
                self.partner,
            )
            self.to_pair[j].start()
        self.copies += self.to_pair

    def pass_on(self):
        self.to_peer = []
        for j in self.order[:-1]:
            peer = self.peer(j)
            self.to_pair[j].wait_recv()
            self.held[j] = low(wide(self.part[peer]) + wide(self.first[j]))
            copy = remote(
                self.held.at[j],
                self.second.at[j],
                self.sems.at[2, j],
                self.sems.at[3, j],
                self.axis,
                peer,
            )
            copy.start()
            self.to_peer.append(copy)
        self.copies += self.to_peer

    def total(self):
        self.to_pair[0].wait_recv()
        total = wide(self.part[self.me]) + wide(self.first[0])
        for j in self.order[:-1]:
            self.to_peer[j - 1].wait_recv()
            total = total + wide(self.second[j])
        return total

    def drain(self):
        for copy in self.copies:
            copy.wait_send()


class Reduce(Scatter):
    def __init__(self, axis, n, part, first, held, second, whole, sems):
        super().__init__(axis, n, part, first, held, second, sems)
        self.whole = whole

    def gather(self):
        mine = self.whole.at[self.me]
        self.around = []
        for j in range(1, self.groups):
            self.around.append(
                remote(mine, mine, self.sems.at[4, j], self.sems.at[5, j], self.axis, self.peer(j))
            )
            self.around[-1].start()
        across = remote(mine, mine, self.sems.at[6, 0], self.sems.at[7, 0], self.axis, self.partner)
        across.start()
        self.across = [across]

    def forward(self):
        for j in range(1, self.groups):
            self.around[j - 1].wait_recv()
            owner = lax.rem(self.group + self.groups - j, self.groups) * 2 + self.parity
            block = self.whole.at[owner]
            copy = remote(
                block, block, self.sems.at[6, j], self.sems.at[7, j], self.axis, self.partner
            )
            copy.start()
            self.across.append(copy)

    def finish(self):
        for copy in self.across:
            copy.wait_recv()
        self.copies += self.around + self.across


def greet(axes):
    barrier = pltpu.get_barrier_semaphore()
    count = 0
    for axis, n in axes:
        _, parity, group, partner, groups = place(axis, n)
        others = [partner]
        for j in range(1, groups):
            others.append(lax.rem(group + j, groups) * 2 + parity)
        for other in others:
            pl.semaphore_signal(barrier, inc=1, device_id={axis: other}, device_id_type=MESH)
        count += len(others)
    return count


def kernel(
    n,
    m,
    lengths,
    tokens,
    cotangent,
    triple_hbm,
    output_hbm,
    upward_hbm,
    downward_hbm,
    final_hbm,
    triple_out_hbm,
    output_out_hbm,
    upward_out_hbm,
    downward_out_hbm,
    triple_weight,
    output_weight,
    upward_weight,
    downward_weight,
    triple_out,
    output_out,
    upward_out,
    downward_out,
    in_sems,
    out_sems,
    final_sem,
    part,
    first,
    held,
    second,
    whole,
    sems,
    down_part,
    down_first,
    down_held,
    down_second,
    down_sems,
    up_part,
    up_first,
    up_held,
    up_second,
    up_sems,
    att_part,
    att_first,
    att_held,
    att_second,
    att_sems,
    qkv_part,
    qkv_first,
    qkv_held,
    qkv_second,
    qkv_sems,
    normed,
    qkv,
    probs,
    context,
    normed_mid,
    slope,
    activated,
    grad_act,
    grad_preact,
    grad_context,
    grad_qkv,
):
    pairs = (
        (triple_hbm, triple_weight),
        (output_hbm, output_weight),
        (upward_hbm, upward_weight),
        (downward_hbm, downward_weight),
    )
    loads = [
        [pltpu.make_async_copy(far.at[l], near.at[l], in_sems.at[l, i]) for i, (far, near) in enumerate(pairs)]
        for l in range(LAYERS)
    ]
    for layer_loads in loads:
        for copy in layer_loads:
            copy.start()
    greeted = greet((("mp", n), ("dp", m)))
    halves, _, chunk, width = tokens.shape
    half_rows = n * chunk
    row_count = halves * half_rows
    slates = row_count // SLATE
    held_cols = output_weight.shape[-1]
    heads = held_cols // HD
    me = lax.axis_index("mp")
    query_rows = min(SLATE, half_rows)
    position = lax.broadcasted_iota(jnp.int32, (1, SLATE), 1)

    def rows(ref):
        return ref[...].reshape(row_count, width)

    def half(ref, a):
        return ref[a].reshape(half_rows, width)

    def cut(a):
        return slice(a * half_rows, (a + 1) * half_rows)

    def opened(k, a, value):
        part[k, a] = low(value).reshape(n, chunk, width)
        return reducer(k, a)

    def reducer(k, a):
        refs = [ref.at[k, a] for ref in (part, first, held, second, whole, sems)]
        return Reduce("mp", n, *refs)

    def scatterer(refs, l):
        return Scatter("dp", m, *[ref.at[l] for ref in refs])

    def grad_work(ref, l, left, right, scatter):
        share = width // m

        def piece(d):
            columns = slice(d * share, (d + 1) * share)
            ref[l, d] = low(contract_rows(left(columns), right()))
            if d == m - 1:
                scatter.start()

        return [functools.partial(piece, d) for d in range(m)]

    def rows_of(ref):
        return lambda columns: ref[:, :, :, columns].reshape(row_count, -1)

    def slices(s, h):
        block = slice(s * SLATE, (s + 1) * SLATE)
        return block, [slice(i * held_cols + h * HD, i * held_cols + (h + 1) * HD) for i in range(3)]

    def joined(l):
        return jnp.concatenate([triple_weight[l, i] for i in range(3)], axis=-1)

    drained = []
    span = range(halves)

    def close(k, steps, own, work=()):
        work = list(work)
        each = -(-len(work) // (3 * halves))

        def tick():
            for _ in range(min(each, len(work))):
                work.pop(0)()

        for step in steps:
            tick()
            step.pass_on()
        for a in span:
            tick()
            whole[k, a, me] = low(own(a, steps[a].total()))
            steps[a].gather()
        for step in steps:
            tick()
            step.forward()
        drained.extend(steps)

    def added(stream):
        return lambda a, total: wide(stream[a, me]) + total

    def normed_back(stream, upstream):
        def own(a, total):
            _, scaled, rscale = normalize(stream[a, me])
            return wide(upstream[a, me]) + norm_backward(scaled, rscale, total)

        return own

    stream = tokens
    arriving = None
    streams, mids = [], []
    for l in range(LAYERS):
        streams.append(stream)
        loads[l][0].wait()
        for a in span:
            if arriving is not None:
                arriving[a].finish()
            normed[l, cut(a)] = normalize(half(stream, a))[0]
            qkv[l, cut(a)] = low(dot(normed[l, cut(a)], joined(l)))
        loads[l][1].wait()
        k_here = 2 * l
        steps = []
        for a in span:
            for start in range(a * half_rows, (a + 1) * half_rows, query_rows):
                s, offset = start // SLATE, start % SLATE
                live = wide(position < lengths[s])
                block = slice(start, start + query_rows)
                for h in range(heads):
                    keys, (q, k, v) = slices(s, h)
                    scores = contract_cols(qkv[l, block, q], qkv[l, keys, k]) * HD ** (-0.5)
                    weights = jnp.exp(scores) * live
                    share = weights / jnp.sum(weights, axis=-1, keepdims=True)
                    probs[l, s * heads + h, offset : offset + query_rows] = share
                    context[l, block, h * HD : (h + 1) * HD] = low(
                        dot(low(share), qkv[l, keys, v])
                    )
            steps.append(opened(k_here, a, contract_cols(context[l, cut(a)], output_weight[l])))
            if l == 0 and a == 0:
                pl.semaphore_wait(pltpu.get_barrier_semaphore(), greeted)
            steps[a].start()

        def early(l=l):
            loads[l][2].wait()
            loads[l][3].wait()
            if l == LAYERS - 1:
                for a in span:
                    grad_act[cut(a)] = low(dot(half(cotangent, a), downward_weight[l]))

        close(k_here, steps, added(stream), [early])
        mid = whole.at[k_here]
        mids.append(mid)
        if l == LAYERS - 1:
            break
        nexts = []
        for a in span:
            steps[a].finish()
            normed_mid[l, cut(a)] = normalize(half(mid, a))[0]
            preact = dot(normed_mid[l, cut(a)], upward_weight[l])
            activated[l, cut(a)] = low(gate(preact))
            nexts.append(
                opened(k_here + 1, a, contract_cols(activated[l, cut(a)], downward_weight[l]))
            )
            nexts[a].start()
            slope[l, cut(a)] = gate_slope(preact)
        close(k_here + 1, nexts, added(mid))
        stream = whole.at[k_here + 1]
        arriving = nexts

    final_k = 2 * LAYERS - 1
    finals = [reducer(final_k, a) for a in span]
    final_copy = pltpu.make_async_copy(whole.at[final_k], final_hbm, final_sem)

    def final_gather():
        for a in span:
            whole[final_k, a, me] = low(wide(mids[-1][a, me]) + finals[a].total())
            finals[a].gather()

    def final_finish():
        for item in finals:
            item.finish()
        final_copy.start()

    def each(name):
        def act():
            for item in finals:
                getattr(item, name)()

        return act

    later = [each("start"), each("pass_on"), final_gather, each("forward"), final_finish]

    def advance():
        if later:
            later.pop(0)()

    stores = [final_copy]

    def store(i, l, near, far):
        copy = pltpu.make_async_copy(near.at[l], far.at[l], out_sems.at[l, i])
        copy.start()
        stores.append(copy)

    def triple_done(scatter, l):
        total = scatter.total()
        for i in range(3):
            triple_out[l, i] = total[:, i * held_cols : (i + 1) * held_cols]
        store(0, l, triple_out, triple_out_hbm)

    def output_done(scatter, l):
        output_out[l] = scatter.total()
        store(1, l, output_out, output_out_hbm)

    def upward_done(scatter, l):
        upward_out[l] = scatter.total()
        store(2, l, upward_out, upward_out_hbm)

    def downward_done(scatter, l):
        downward_out[l] = scatter.total()
        store(3, l, downward_out, downward_out_hbm)

    pending = []

    def flush():
        while pending:
            pending.pop(0)()

    upstream = cotangent
    arriving = steps
    k_next = 2 * LAYERS
    for l in reversed(range(LAYERS)):
        last = l == LAYERS - 1
        steps = []
        for a in span:
            arriving[a].finish()
            if last:
                normed_mid[l, cut(a)] = normalize(half(mids[l], a))[0]
                preact = dot(normed_mid[l, cut(a)], upward_weight[l])
                slope[l, cut(a)] = gate_slope(preact)
                act_back = grad_act[cut(a)]
            else:
                act_back = low(dot(half(upstream, a), downward_weight[l]))
            grad_preact[l, cut(a)] = low(wide(act_back) * slope[l, cut(a)])
            steps.append(
                opened(k_next, a, contract_cols(grad_preact[l, cut(a)], upward_weight[l]))
            )
            steps[a].start()
            if last:
                activated[l, cut(a)] = low(gate(preact))
        down = scatterer((down_part, down_first, down_held, down_second, down_sems), l)
        up = scatterer((up_part, up_first, up_held, up_second, up_sems), l)
        att = scatterer((att_part, att_first, att_held, att_second, att_sems), l)
        triple = scatterer((qkv_part, qkv_first, qkv_held, qkv_second, qkv_sems), l)
        drained += [down, up, att, triple]

        def feed_final(a, l=l):
            opened(final_k, a, contract_cols(activated[l, cut(a)], downward_weight[l]))

        work = grad_work(down_part, l, rows_of(upstream), lambda l=l: activated[l], down)
        work += grad_work(
            up_part, l, lambda c, l=l: normed_mid[l, :, c], lambda l=l: grad_preact[l], up
        )
        work.append(down.pass_on)
        if last:
            work += [functools.partial(feed_final, a) for a in span]
        close(k_next, steps, normed_back(mids[l], upstream), work)
        grad_mid = whole.at[k_next]
        k_next += 1
        for a in span:
            steps[a].finish()
            grad_context[cut(a)] = low(dot(half(grad_mid, a), output_weight[l]))
        up.pass_on()
        advance()
        for s in range(slates):
            for h in range(heads):
                block, (q, k, v) = slices(s, h)
                share = probs[l, s * heads + h]
                back = grad_context[block, h * HD : (h + 1) * HD]
                grad_prob = contract_cols(back, qkv[l, block, v])
                grad_qkv[l, block, v] = low(contract_rows(low(share), back))
                inner = jnp.sum(grad_prob * share, axis=-1, keepdims=True)
                grad_score = low(share * (grad_prob - inner) * HD ** (-0.5))
                grad_qkv[l, block, q] = low(dot(grad_score, qkv[l, block, k]))
                grad_qkv[l, block, k] = low(contract_rows(grad_score, qkv[l, block, q]))

        att_work = grad_work(
            att_part, l, rows_of(grad_mid), lambda l=l: context[l], att
        )
        triple_work = grad_work(
            qkv_part, l, lambda c, l=l: normed[l, :, c], lambda l=l: grad_qkv[l], triple
        )
        if l > 0:
            steps = []
            for a in span:
                steps.append(opened(k_next, a, contract_cols(grad_qkv[l, cut(a)], joined(l))))
                steps[a].start()
            work = triple_work + att_work + [advance, triple.pass_on, att.pass_on]
            close(k_next, steps, normed_back(streams[l], grad_mid), work)
            arriving = steps
            upstream = whole.at[k_next]
            k_next += 1
            pending.append(functools.partial(downward_done, down, l))
            pending.append(functools.partial(upward_done, up, l))
            pending.append(functools.partial(output_done, att, l))
            pending.append(functools.partial(triple_done, triple, l))
        else:
            for item in triple_work + att_work:
                item()
            advance()
            triple.pass_on()
            att.pass_on()
            advance()
            flush()
            downward_done(down, l)
            upward_done(up, l)
            while later:
                advance()
            output_done(att, l)
            triple_done(triple, l)
    drained += finals
    for item in drained:
        item.drain()
    for copy in stores:
        copy.wait()


def hand_over(*refs):
    count = (len(refs) - 1) // 3
    sources, targets, staged, sems = refs[:count], refs[count : 2 * count], refs[2 * count : -1], refs[-1]
    pairs = [(i, j) for i in range(count) for j in range(sources[i].shape[0])]
    ins = [pltpu.make_async_copy(sources[i].at[j], staged[i].at[j], sems.at[0, i, j]) for i, j in pairs]
    outs = [pltpu.make_async_copy(staged[i].at[j], targets[i].at[j], sems.at[1, i, j]) for i, j in pairs]
    for copy in ins:
        copy.start()
    for copy, onward in zip(ins, outs):
        copy.wait()
        onward.start()
    for copy in outs:
        copy.wait()


def body(
    n, m, tokens, lengths, cotangent, triple_weight, output_weight, upward_weight, downward_weight
):
    row_count, width = tokens.shape
    halves = 2 if (row_count // n) % 32 == 0 else 1
    chunk = row_count // (n * halves)
    share = width // m
    held_cols = output_weight.shape[-1]
    hidden = upward_weight.shape[-1]
    triple_cols = 3 * held_cols
    heads_all = (row_count // SLATE) * (held_cols // HD)
    sums = 2 * LAYERS + 2 * LAYERS - 1
    vmem = pl.BlockSpec(memory_space=pltpu.VMEM)
    smem = pl.BlockSpec(memory_space=pltpu.SMEM)
    anywhere = pl.BlockSpec(memory_space=pl.ANY)
    bf16, f32 = jnp.bfloat16, jnp.float32
    whole = (halves, n, chunk, width)
    weights = (
        triple_weight.transpose(0, 2, 1, 3),
        output_weight,
        upward_weight,
        downward_weight,
    )
    results = [
        jax.ShapeDtypeStruct(whole, bf16),
        jax.ShapeDtypeStruct((LAYERS, 3, share, held_cols), f32),
        jax.ShapeDtypeStruct((LAYERS, share, held_cols), f32),
        jax.ShapeDtypeStruct((LAYERS, share, hidden), f32),
        jax.ShapeDtypeStruct((LAYERS, share, hidden), f32),
    ]

    def grads(columns):
        part = (LAYERS, m, share, columns)
        half = pltpu.VMEM((LAYERS, m // 2, share, columns), bf16)
        return [pltpu.VMEM(part, bf16), half, half, half, pltpu.SemaphoreType.DMA((LAYERS, 4, m // 2))]

    half = pltpu.VMEM((sums, halves, n // 2, chunk, width), bf16)
    full = pltpu.VMEM((sums,) + whole, bf16)
    outs = pl.pallas_call(
        functools.partial(kernel, n, m),
        out_shape=results,
        in_specs=[smem, vmem, vmem] + [anywhere] * 4,
        out_specs=[anywhere] * 5,
        scratch_shapes=[pltpu.VMEM(weight.shape, bf16) for weight in weights]
        + [pltpu.VMEM(result.shape, f32) for result in results[1:]]
        + [
            pltpu.SemaphoreType.DMA((LAYERS, 4)),
            pltpu.SemaphoreType.DMA((LAYERS, 4)),
            pltpu.SemaphoreType.DMA,
        ]
        + [full, half, half, half, full, pltpu.SemaphoreType.DMA((sums, halves, 8, n // 2))]
        + grads(hidden)
        + grads(hidden)
        + grads(held_cols)
        + grads(triple_cols)
        + [
            pltpu.VMEM((LAYERS, row_count, width), bf16),
            pltpu.VMEM((LAYERS, row_count, triple_cols), bf16),
            pltpu.VMEM((LAYERS, heads_all, SLATE, SLATE), f32),
            pltpu.VMEM((LAYERS, row_count, held_cols), bf16),
            pltpu.VMEM((LAYERS, row_count, width), bf16),
            pltpu.VMEM((LAYERS, row_count, hidden), f32),
            pltpu.VMEM((LAYERS, row_count, hidden), bf16),
            pltpu.VMEM((row_count, hidden), bf16),
            pltpu.VMEM((LAYERS, row_count, hidden), bf16),
            pltpu.VMEM((row_count, held_cols), bf16),
            pltpu.VMEM((LAYERS, row_count, triple_cols), bf16),
        ],
        compiler_params=pltpu.CompilerParams(
            collective_id=0, has_side_effects=True, vmem_limit_bytes=60 << 20
        ),
    )(lengths, tokens.reshape(whole), cotangent.reshape(whole), *weights)
    most = max(result.shape[0] for result in results)
    final, triple, output, upward, downward = pl.pallas_call(
        hand_over,
        out_shape=results,
        in_specs=[anywhere] * 5,
        out_specs=[anywhere] * 5,
        scratch_shapes=[pltpu.VMEM(result.shape, result.dtype) for result in results]
        + [pltpu.SemaphoreType.DMA((2, 5, most))],
    )(*outs)
    return (
        final.reshape(row_count, width),
        triple.transpose(0, 2, 1, 3),
        output,
        upward,
        downward,
    )


def solution(mesh):
    placed = (
        P("dp", None),
        P("dp"),
        P("dp", None),
        P(None, None, None, "mp"),
        P(None, None, "mp"),
        P(None, None, "mp"),
        P(None, None, "mp"),
    )
    return jax.shard_map(
        functools.partial(body, mesh.shape["mp"], mesh.shape["dp"]),
        mesh=mesh,
        in_specs=placed,
        out_specs=(
            P("dp", None),
            P(None, "dp", None, "mp"),
            P(None, "dp", "mp"),
            P(None, "dp", "mp"),
            P(None, "dp", "mp"),
        ),
        check_vma=False,
    )
```
